128 devices in a mesh: shard: 16 (over y, z), context: 2 (over x_lo), tensor: 4 (over x_hi, core).
Axes of the slice: x: 4 (x_hi: 2, x_lo: 2; x = x_hi * 2 + x_lo), y: 4, z: 4, core: 2. Of those that a mesh axis runs over, the one named last changes fastest.
Arguments:
- tokens: bfloat16 [16, 1024, 1024], P('shard', ('context', 'tensor')), may hold values from -6 to 6
- cotangent: bfloat16 [16, 1024, 1024], P('shard', ('context', 'tensor')), may hold values from -6 to 6
- attention_gain: bfloat16 [1024], P('shard'), may hold values from 0.099609375 to 1.8984375
- query_weight: bfloat16 [1024, 1024], P('shard'), may hold values from -0.1875 to 0.1875
- key_weight: bfloat16 [1024, 512], P('shard'), may hold values from -0.1875 to 0.1875
- value_weight: bfloat16 [1024, 512], P('shard'), may hold values from -0.1875 to 0.1875
- query_gain: bfloat16 [64], P('shard'), may hold values from 0.099609375 to 1.8984375
- key_gain: bfloat16 [64], P('shard'), may hold values from 0.099609375 to 1.8984375
- out_weight: bfloat16 [1024, 1024], P('shard'), may hold values from -0.375 to 0.375
- feed_gain: bfloat16 [1024], P('shard'), may hold values from 0.099609375 to 1.8984375
- gate_weight: bfloat16 [1024, 4608], P('shard', 'tensor'), may hold values from -0.1875 to 0.1875
- up_weight: bfloat16 [1024, 4608], P('shard', 'tensor'), may hold values from -0.1875 to 0.1875
- down_weight: bfloat16 [4608, 1024], P('tensor', 'shard'), may hold values from -0.09375 to 0.09375
Outputs:
- output: bfloat16 [16, 1024, 1024], P('shard', ('context', 'tensor'))
- input_gradient: bfloat16 [16, 1024, 1024], P('shard', ('context', 'tensor'))
- attention_gain_gradient: float32 [1024], P('shard')
- query_weight_gradient: float32 [1024, 1024], P('shard')
- key_weight_gradient: float32 [1024, 512], P('shard')
- value_weight_gradient: float32 [1024, 512], P('shard')
- query_gain_gradient: float32 [64], P('shard')
- key_gain_gradient: float32 [64], P('shard')
- out_weight_gradient: float32 [1024, 1024], P('shard')
- feed_gain_gradient: float32 [1024], P('shard')
- gate_weight_gradient: float32 [1024, 4608], P('shard', 'tensor')
- up_weight_gradient: float32 [1024, 4608], P('shard', 'tensor')
- down_weight_gradient: float32 [4608, 1024], P('tensor', 'shard')
The draws below stay inside these ranges and needn't reach their ends.
All inputs are finite; a program needn't handle non-finite values.
Results may differ from the reference program's by a relative error of at most 0.015.
Values may be sent and summed in bfloat16 or wider, within the bound.
No kernel may reach another device: no remote copies, remote signals or barrier semaphores. Data moves between devices by JAX's collectives and lax.ppermute only.
A program may use at most 128 MiB of HBM per device.

```python
import jax
import jax.numpy as jnp
from jax import lax

D = 1024
HQ = 16
KV = 8
HD = 64
FF = 4608
LEN = 1024
SEQUENCES = 16


def levels(stream_key, extent, pieces, smallest, largest):
    def one(dim, blocks):
        draws = jax.random.uniform(jax.random.fold_in(jax.random.fold_in(stream_key, 6), dim), (blocks,), jnp.float32, smallest / len(pieces), largest / len(pieces))
        return jnp.repeat(jnp.exp(draws), extent[dim] // blocks).reshape((-1,) + (1,) * (len(extent) - dim - 1))

    level = one(*pieces[0])
    for cut in pieces[1:]:
        level = level * one(*cut)
    return level


def bell_draw(key, shape, deviation, limit, pieces=(), held_as=jnp.bfloat16):
    drawn = jax.random.normal(key, shape, jnp.float32) * deviation
    if len(pieces) > 0:
        drawn = levels(key, shape, pieces, -0.22, 0.18) * drawn
    return jnp.clip(drawn, min=-limit, max=limit).astype(held_as)


def setup_inputs(seed: int = 0) -> dict:
    key_list = jax.random.split(jax.random.key(seed), 14)
    tokens = bell_draw(key_list[0], (SEQUENCES, LEN, D), 1.0, 6.0, ((0, 16), (1, 8)))
    cotangent = bell_draw(key_list[1], (SEQUENCES, LEN, D), 1.0, 6.0, ((0, 16), (1, 8)))
    attention_gain = jnp.clip(1.0 + 0.18 * jax.random.normal(key_list[2], (D,), jnp.float32), 0.099609375, 1.8984375).astype(jnp.bfloat16)
    query_weight = bell_draw(key_list[3], (D, HQ * HD), D ** -0.5, 0.1875, ((0, 16),))
    key_weight = bell_draw(key_list[4], (D, KV * HD), D ** -0.5, 0.1875, ((0, 16),))
    value_weight = bell_draw(key_list[5], (D, KV * HD), D ** -0.5, 0.1875, ((0, 16),))
    query_gain = jnp.clip(1.0 + 0.18 * jax.random.normal(key_list[6], (HD,), jnp.float32), 0.099609375, 1.8984375).astype(jnp.bfloat16)
    key_gain = jnp.clip(1.0 + 0.18 * jax.random.normal(key_list[7], (HD,), jnp.float32), 0.099609375, 1.8984375).astype(jnp.bfloat16)
    out_weight = bell_draw(key_list[8], (HQ * HD, D), (HQ * HD // 4) ** -0.5, 0.375, ((0, 16),))
    feed_gain = jnp.clip(1.0 + 0.18 * jax.random.normal(key_list[9], (D,), jnp.float32), 0.099609375, 1.8984375).astype(jnp.bfloat16)
    gate_weight = bell_draw(key_list[10], (D, FF), D ** -0.5, 0.1875, ((0, 16), (1, 4)))
    up_weight = bell_draw(key_list[11], (D, FF), D ** -0.5, 0.1875, ((0, 16), (1, 4)))
    down_weight = bell_draw(key_list[12], (FF, D), FF ** -0.5, 0.09375, ((0, 4), (1, 16)))
    return {"tokens": tokens, "cotangent": cotangent, "attention_gain": attention_gain, "query_weight": query_weight, "key_weight": key_weight, "value_weight": value_weight, "query_gain": query_gain, "key_gain": key_gain, "out_weight": out_weight, "feed_gain": feed_gain, "gate_weight": gate_weight, "up_weight": up_weight, "down_weight": down_weight}


@jax.custom_vjp
def low(v):
    return lax.optimization_barrier(v.astype(jnp.bfloat16)).astype(jnp.float32)

@jax.custom_vjp
def low_back(v):
    return v

def low_keep(v):
    return (low(v), None)

def low_pass(kept, grad):
    return (grad,)

def back_keep(v):
    return (v, None)

def back_low(kept, grad):
    return (low(grad),)
low.defvjp(low_keep, low_pass)
low_back.defvjp(back_keep, back_low)
epsilon = 1e-05
rope_base = 1000000.0
masked_score = -1e+30
precise = lax.Precision.HIGHEST

def rms_scale(value, gain):
    mean_square = lax.optimization_barrier(jnp.mean(value * value, axis=-1, keepdims=True))
    return value * lax.rsqrt(mean_square + epsilon) * gain

def rope_tables(positions, head_dim):
    exponent = jnp.arange(0, head_dim, 2).astype(jnp.float32) / head_dim
    frequency = 1.0 / rope_base ** exponent
    angle = positions.astype(jnp.float32)[:, None] * frequency[None, :]
    angle = jnp.concatenate([angle, angle], axis=-1)
    return (jnp.cos(angle), jnp.sin(angle))

def rotate(value, cosine, sine):
    half = value.shape[-1] // 2
    turned = jnp.concatenate([-value[..., half:], value[..., :half]], axis=-1)
    return value * cosine + turned * sine

def layer(sequence, params):
    attention_gain, query_weight, key_weight, value_weight, query_gain, key_gain, out_weight, feed_gain, gate_weight, up_weight, down_weight = params
    length = sequence.shape[0]
    head_dim = query_gain.shape[0]
    query_heads = query_weight.shape[1] // head_dim
    shared_heads = key_weight.shape[1] // head_dim
    group = query_heads // shared_heads
    mixer_input = low(rms_scale(sequence, attention_gain))
    query_raw = low_back(jnp.dot(mixer_input, query_weight, precision=precise))
    key_raw = low_back(jnp.dot(mixer_input, key_weight, precision=precise))
    values = low_back(low(jnp.dot(mixer_input, value_weight, precision=precise)))
    cosine, sine = rope_tables(jnp.arange(length), head_dim)
    cosine = cosine[:, None, :]
    sine = sine[:, None, :]
    queries = low_back(low(rotate(rms_scale(query_raw.reshape(length, query_heads, head_dim), query_gain), cosine, sine)))
    keys = low_back(low(rotate(rms_scale(key_raw.reshape(length, shared_heads, head_dim), key_gain), cosine, sine)))
    keys_wide = jnp.repeat(keys, group, axis=1)
    values_wide = jnp.repeat(values.reshape(length, shared_heads, head_dim), group, axis=1)
    score = low_back(jnp.einsum('qhd,khd->hqk', queries, keys_wide, precision=precise) * head_dim ** (-0.5))
    allowed = jnp.arange(length)[None, :] <= jnp.arange(length)[:, None]
    score = jnp.where(allowed[None], score, masked_score)
    peak = lax.optimization_barrier(jnp.max(score, axis=-1, keepdims=True))
    raised = jnp.exp(score - peak)
    chance = low(raised / lax.optimization_barrier(jnp.sum(raised, axis=-1, keepdims=True)))
    attended = low_back(low(jnp.einsum('hqk,khd->qhd', chance, values_wide, precision=precise)))
    attended = attended.reshape(length, query_heads * head_dim)
    branch = low_back(jnp.dot(attended, out_weight, precision=precise))
    mixed = sequence + branch
    feed_input = low(rms_scale(mixed, feed_gain))
    gate = low_back(jnp.dot(feed_input, gate_weight, precision=precise))
    upward = low_back(jnp.dot(feed_input, up_weight, precision=precise))
    hidden = low(gate * jax.nn.sigmoid(gate) * upward)
    return mixed + jnp.dot(hidden, down_weight, precision=precise)

def reference(tokens, cotangent, attention_gain, query_weight, key_weight, value_weight, query_gain, key_gain, out_weight, feed_gain, gate_weight, up_weight, down_weight):
    params = (attention_gain.astype(jnp.float32), query_weight.astype(jnp.float32), key_weight.astype(jnp.float32), value_weight.astype(jnp.float32), query_gain.astype(jnp.float32), key_gain.astype(jnp.float32), out_weight.astype(jnp.float32), feed_gain.astype(jnp.float32), gate_weight.astype(jnp.float32), up_weight.astype(jnp.float32), down_weight.astype(jnp.float32))
    inputs = tokens.astype(jnp.float32)
    seeds = cotangent.astype(jnp.float32)

    def one_sequence(totals, pair):
        sequence, seed_rows = pair
        result, pull_back = jax.vjp(layer, sequence, params)
        input_grad, param_grads = pull_back(seed_rows)
        return (jax.tree.map(jnp.add, totals, param_grads), (result, input_grad))
    start_totals = jax.tree.map(jnp.zeros_like, params)
    sums, (outputs, input_grads) = lax.scan(one_sequence, start_totals, (inputs, seeds))
    return (outputs.astype(jnp.bfloat16), input_grads.astype(jnp.bfloat16), sums[0], sums[1], sums[2], sums[3], sums[4], sums[5], sums[6], sums[7], sums[8], sums[9], sums[10])
```

```python
import jax
import jax.numpy as jnp
from jax import lax
from jax.sharding import PartitionSpec as P

epsilon = 1e-05
rope_base = 1000000.0
masked_score = -1e30
line = ("context", "tensor")
f32 = jnp.float32
bf16 = jnp.bfloat16


def rope_tables(positions, head_dim):
    exponent = jnp.arange(0, head_dim, 2).astype(f32) / head_dim
    frequency = 1.0 / rope_base**exponent
    angle = positions.astype(f32)[:, None] * frequency[None, :]
    angle = jnp.concatenate([angle, angle], axis=-1)
    return (jnp.cos(angle), jnp.sin(angle))


def rotate(value, cosine, sine):
    half = value.shape[-1] // 2
    turned = jnp.concatenate([-value[..., half:], value[..., :half]], axis=-1)
    return value * cosine + turned * sine


def rotate_back(grad_value, cosine, sine):
    half = grad_value.shape[-1] // 2
    moved = grad_value * sine
    turned = jnp.concatenate([moved[..., half:], -moved[..., :half]], axis=-1)
    return grad_value * cosine + turned


def rms_parts(value):
    inverse = lax.rsqrt(jnp.mean(value * value, axis=-1, keepdims=True) + epsilon)
    return (value * inverse, inverse)


def norm_back(grad_value, normed, inverse, gain):
    scaled = grad_value * gain
    return inverse * (scaled - normed * jnp.mean(scaled * normed, axis=-1, keepdims=True))


def dot(a, b):
    return jnp.dot(a, b, preferred_element_type=f32)


def dot_nt(a, b):
    return lax.dot_general(a, b, (((1,), (1,)), ((), ())), preferred_element_type=f32)


def dot_tn(a, b):
    return lax.dot_general(a, b, (((0,), (0,)), ((), ())), preferred_element_type=f32)


def swap(value, bits):
    return lax.ppermute(value, line, [(i, i ^ bits) for i in range(8)])


def flips():
    tensor = lax.axis_index("tensor")
    return (tensor % 2 == 1, lax.axis_index("context") == 1, tensor // 2 == 1)


def exchange_bits(value):
    for dim, flag in enumerate(flips()):
        value = jnp.where(flag, jnp.flip(value, dim), value)
    return value


def to_places(value):
    n, w = value.shape[-2:]
    value = exchange_bits(value.reshape(2, 2, 2, n, w))
    return jnp.moveaxis(value, 0, 2).reshape(8 * n, w)


def to_partners(value):
    n, w = value.shape[0] // 8, value.shape[1]
    value = jnp.moveaxis(value.reshape(2, 2, 2, n, w), 2, 0)
    return exchange_bits(value).reshape(2, 4, n, w)


def line_gather(block):
    mine = jnp.stack([block, swap(block, 2), swap(block, 4), swap(block, 6)])
    other = swap(mine, 1)
    return jnp.stack([mine, other])


def line_reduce(parts):
    low = parts.astype(bf16)
    summed = parts[0] + swap(low[1], 1).astype(f32)
    sent = summed.astype(bf16)
    total = summed[0]
    for chip in (2, 1, 3):
        total = total + swap(sent[chip], 2 * chip).astype(f32)
    return total


def line_turn(parts):
    got = swap(parts[1], 1)
    both = jnp.stack([parts[0], got], axis=1)
    arrived = [both[0]] + [swap(both[chip], 2 * chip) for chip in (1, 2, 3)]
    return jnp.stack(arrived, axis=1)


def on_device(
    tokens,
    cotangent,
    attention_gain,
    query_weight,
    key_weight,
    value_weight,
    query_gain,
    key_gain,
    out_weight,
    feed_gain,
    gate_weight,
    up_weight,
    down_weight,
):
    _, piece, width = tokens.shape
    shard_count = lax.axis_size("shard")
    rows = query_weight.shape[0]
    head_dim = query_gain.shape[0] * shard_count
    length = piece * 8
    context = lax.axis_index("context")
    place = context * lax.axis_size("tensor") + lax.axis_index("tensor")
    heads_width = query_weight.shape[1] // 8
    half = gate_weight.shape[1] // 2
    scale = head_dim ** (-0.5)

    def my_half(value, axis):
        return lax.dynamic_slice_in_dim(value, context * half, half, axis)

    feed_pack = jnp.concatenate(
        [my_half(gate_weight, 1), my_half(up_weight, 1), my_half(down_weight, 0).T], axis=1
    )
    feed_full = lax.all_gather(feed_pack, "shard", axis=0, tiled=True)

    def mine(value, size):
        return lax.dynamic_slice_in_dim(value, place * size, size, 1)

    extra = jnp.zeros((16, 3 * heads_width), bf16)
    gain_rows = jnp.stack([attention_gain, feed_gain])
    extra = extra.at[:2, :rows].set(gain_rows)
    extra = extra.at[2, : head_dim // shard_count].set(query_gain)
    extra = extra.at[3, : head_dim // shard_count].set(key_gain)
    pack = jnp.concatenate(
        [
            mine(query_weight, heads_width),
            mine(key_weight, head_dim),
            mine(value_weight, head_dim),
            mine(out_weight, heads_width),
        ],
        axis=1,
    )
    pack = jnp.concatenate([pack, extra], axis=0)
    pack_all = lax.all_to_all(
        jnp.broadcast_to(pack[None], (shard_count,) + pack.shape), "shard", 0, 0, tiled=True
    )
    weights = pack_all[:, :rows].reshape(width, 3 * heads_width)
    qkv_weight = weights[:, : 2 * heads_width]
    out_columns = weights[:, 2 * heads_width :]
    gains = pack_all[:, rows:].astype(f32)
    gain_first = gains[:, 0, :rows].reshape(-1)
    gain_second = gains[:, 1, :rows].reshape(-1)
    gain_query = gains[:, 2, : head_dim // shard_count].reshape(-1)
    gain_key = gains[:, 3, : head_dim // shard_count].reshape(-1)

    token_rows = tokens.reshape(piece, width)
    seed_rows = cotangent.reshape(piece, width)
    tokens_all = line_gather(token_rows).reshape(length, width)
    normed_all, _ = rms_parts(tokens_all.astype(f32))
    mixer_input = (normed_all * gain_first).astype(bf16)
    raw = dot(mixer_input, qkv_weight)
    raw = to_places(raw.reshape(2, 4, piece, 2 * heads_width))
    cosine, sine = rope_tables(jnp.arange(length), head_dim)
    query_raw = raw[:, :heads_width].reshape(length, 2, head_dim)
    key_raw = raw[:, heads_width : heads_width + head_dim]
    values = raw[:, heads_width + head_dim :].astype(bf16)
    normed_query, inverse_query = rms_parts(query_raw)
    normed_key, inverse_key = rms_parts(key_raw)
    queries = rotate(normed_query * gain_query, cosine[:, None], sine[:, None]).astype(bf16)
    keys = rotate(normed_key * gain_key, cosine, sine).astype(bf16)
    out_partner = line_gather(out_columns)

    block = 512
    starts = list(range(0, length, block))

    def scores(start):
        stop = start + block
        score = (
            jnp.einsum(
                "qhd,kd->hqk", queries[start:stop], keys[:stop], preferred_element_type=f32
            )
            * scale
        )
        allowed = jnp.arange(stop)[None, :] <= (start + jnp.arange(block))[:, None]
        return jnp.where(allowed, score, masked_score)

    results = []
    log_sums = []
    for start in starts:
        score = scores(start)
        peak = jnp.max(score, axis=-1, keepdims=True)
        raised = jnp.exp(score - peak)
        total = jnp.sum(raised, axis=-1, keepdims=True)
        chance = (raised / total).astype(bf16)
        results.append(
            jnp.einsum(
                "hqk,kd->qhd", chance, values[: start + block], preferred_element_type=f32
            ).astype(bf16)
        )
        log_sums.append(peak + jnp.log(total))
    attended_heads = jnp.concatenate(results, axis=0).reshape(length, heads_width)
    attended_turned = line_turn(to_partners(attended_heads))
    attended = to_places(attended_turned).reshape(8, piece, heads_width)
    attended = jnp.moveaxis(attended, 0, 1).reshape(piece, width)

    out_wide = jnp.moveaxis(out_partner.reshape(8, width, heads_width), 0, 1).reshape(width, width)
    branch = dot(attended, out_wide).reshape(piece, 8, heads_width)
    branch = to_places(jnp.moveaxis(branch, 1, 0).reshape(2, 4, piece, heads_width))
    branch = jnp.moveaxis(branch.reshape(8, piece, heads_width), 0, 1).reshape(piece, width)
    mixed = token_rows.astype(f32) + branch
    normed_second, inverse_second = rms_parts(mixed)
    feed_input = (normed_second * gain_second).astype(bf16)

    seed_all = line_gather(seed_rows).reshape(length, width)
    feed_all = line_gather(feed_input).reshape(length, width)
    gate_full = feed_full[:, :half]
    up_full = feed_full[:, half : 2 * half]
    down_full = feed_full[:, 2 * half :]
    grad_hidden = dot(seed_all, down_full)
    gate = dot(feed_all, gate_full)
    upward = dot(feed_all, up_full)
    squashed = jax.nn.sigmoid(gate)
    activated = gate * squashed
    hidden = (activated * upward).astype(bf16)
    grad_gate = (grad_hidden * upward * squashed * (1.0 + gate * (1.0 - squashed))).astype(bf16)
    grad_up = (grad_hidden * activated).astype(bf16)
    grad_feed = dot_nt(grad_gate, gate_full) + dot_nt(grad_up, up_full)
    grad_feed = line_reduce(grad_feed.reshape(2, 4, piece, width))
    feed_rows = line_reduce(dot_nt(hidden, down_full).reshape(2, 4, piece, width))
    output = (mixed + feed_rows).astype(bf16).reshape(1, piece, width)

    feed_sums = jnp.concatenate(
        [dot_tn(feed_all, grad_gate), dot_tn(feed_all, grad_up), dot_tn(seed_all, hidden)], axis=1
    ).astype(bf16)
    feed_parts = lax.all_to_all(
        feed_sums.reshape(shard_count, rows, 3 * half), "shard", 0, 0, tiled=True
    )
    feed_total = jnp.sum(feed_parts.astype(f32), axis=0)
    feed_other = swap(feed_total.astype(bf16), 4).astype(f32)
    first = jnp.where(context == 0, feed_total, feed_other)
    second = jnp.where(context == 0, feed_other, feed_total)

    def joined(index):
        span = slice(index * half, (index + 1) * half)
        return jnp.concatenate([first[:, span], second[:, span]], axis=1)

    gate_part = joined(0)
    up_part = joined(1)
    down_part = joined(2).T

    grad_mixed = seed_rows.astype(f32) + norm_back(
        grad_feed, normed_second, inverse_second, gain_second
    )
    grad_branch = grad_mixed.astype(bf16)
    branch_all = line_gather(grad_branch).reshape(length, width)
    out_rows = lax.dynamic_slice_in_dim(out_partner, place * heads_width, heads_width, 2)
    out_rows = to_places(out_rows).reshape(8, heads_width, heads_width)
    out_rows = jnp.moveaxis(out_rows, 0, 1).reshape(heads_width, width)
    grad_attended = dot_nt(branch_all, out_rows).astype(bf16)
    attended_partner = to_partners(attended_heads).reshape(length, heads_width)
    out_sum = dot_tn(attended_partner, branch_all).astype(bf16)
    out_sum = jnp.moveaxis(out_sum.reshape(heads_width, 8, heads_width), 1, 0)
    out_turned = line_turn(to_partners(out_sum.reshape(8 * heads_width, heads_width)))
    out_sum = to_places(out_turned)
    grad_heads = to_places(grad_attended.reshape(2, 4, piece, heads_width)).reshape(
        length, 2, head_dim
    )

    key_grad = jnp.zeros((length, head_dim), f32)
    value_grad = jnp.zeros((length, head_dim), f32)
    query_blocks = []
    for index, start in enumerate(starts):
        stop = start + block
        query_block = queries[start:stop]
        grad_block = grad_heads[start:stop]
        chance_full = jnp.exp(scores(start) - log_sums[index])
        grad_chance = jnp.einsum(
            "qhd,kd->hqk", grad_block, values[:stop], preferred_element_type=f32
        )
        inner = jnp.sum(chance_full * grad_chance, axis=-1, keepdims=True)
        grad_score = (chance_full * (grad_chance - inner)).astype(bf16)
        query_blocks.append(
            jnp.einsum("hqk,kd->qhd", grad_score, keys[:stop], preferred_element_type=f32) * scale
        )
        key_grad = key_grad.at[:stop].add(
            jnp.einsum("hqk,qhd->kd", grad_score, query_block, preferred_element_type=f32) * scale
        )
        value_grad = value_grad.at[:stop].add(
            jnp.einsum(
                "hqk,qhd->kd", chance_full.astype(bf16), grad_block, preferred_element_type=f32
            )
        )

    def rounded(value):
        return value.astype(bf16).astype(f32)

    grad_query_normed = rotate_back(
        rounded(jnp.concatenate(query_blocks, axis=0)), cosine[:, None], sine[:, None]
    )
    grad_key_normed = rotate_back(rounded(key_grad), cosine, sine)
    query_gain_sum = jnp.sum(grad_query_normed * normed_query, axis=(0, 1))
    key_gain_sum = jnp.sum(grad_key_normed * normed_key, axis=0)
    grad_raw = jnp.concatenate(
        [
            norm_back(grad_query_normed, normed_query, inverse_query, gain_query).reshape(
                length, heads_width
            ),
            norm_back(grad_key_normed, normed_key, inverse_key, gain_key),
            value_grad,
        ],
        axis=1,
    ).astype(bf16)
    grad_raw = to_partners(grad_raw).reshape(length, 2 * heads_width)
    grad_mixer = line_reduce(dot_nt(grad_raw, qkv_weight).reshape(2, 4, piece, width))
    qkv_sum = dot_tn(mixer_input, grad_raw).astype(bf16)
    normed_first, inverse_first = rms_parts(token_rows.astype(f32))
    input_gradient = (
        (grad_mixed + norm_back(grad_mixer, normed_first, inverse_first, gain_first))
        .astype(bf16)
        .reshape(1, piece, width)
    )

    per_shard = head_dim // shard_count
    last = jnp.zeros((shard_count, 16, 3 * heads_width), bf16)

    def low_pair(value):
        high = value.astype(bf16)
        return jnp.stack([high, (value - high.astype(f32)).astype(bf16)])

    gain_pairs = jnp.concatenate([low_pair(query_gain_sum), low_pair(key_gain_sum)])
    gain_pairs = jnp.moveaxis(gain_pairs.reshape(4, shard_count, per_shard), 0, 1)
    last = last.at[:, :4, :per_shard].set(gain_pairs)
    sums = jnp.concatenate([qkv_sum, out_sum], axis=1).reshape(shard_count, rows, 3 * heads_width)
    sums = jnp.concatenate([sums, last], axis=1)
    parts = lax.all_to_all(sums, "shard", 0, 0, tiled=True)
    total = jnp.sum(parts.astype(f32), axis=0)
    attention_total = total[:rows]
    gain_total = total[rows : rows + 4, :per_shard]
    gain_total = gain_total.reshape(2, 2, per_shard).sum(1)

    def product_sum(weight, grad):
        return jnp.sum(weight.astype(f32) * grad, axis=1)

    first_partial = product_sum(pack[:rows, : 2 * heads_width], attention_total[:, : 2 * heads_width])
    feed_partial = product_sum(feed_pack[:, : 2 * half], feed_total[:, : 2 * half])
    tail = jnp.zeros((16, 3 * heads_width), f32)
    tail = tail.at[0, :rows].set(first_partial).at[1, :rows].set(feed_partial)
    tail = tail.at[2:4, :per_shard].set(gain_total)
    final = jnp.concatenate([attention_total, tail], axis=0)
    final_all = to_places(line_gather(final.astype(bf16))).reshape(8, rows + 16, 3 * heads_width)
    final_all = final_all.astype(f32)

    def columns(low, high):
        return jnp.moveaxis(final_all[:, :rows, low:high], 0, 1).reshape(rows, -1)

    query_part = columns(0, heads_width)
    key_part = columns(heads_width, heads_width + head_dim)
    value_part = columns(heads_width + head_dim, 2 * heads_width)
    out_part = columns(2 * heads_width, 3 * heads_width)
    tails = jnp.sum(final_all[:, rows:], axis=0)
    first_gain_grad = tails[0, :rows] / attention_gain.astype(f32)
    feed_gain_grad = tails[1, :rows] / feed_gain.astype(f32)
    query_gain_grad = tails[2, :per_shard]
    key_gain_grad = tails[3, :per_shard]
    return (
        output,
        input_gradient,
        first_gain_grad,
        query_part,
        key_part,
        value_part,
        query_gain_grad,
        key_gain_grad,
        out_part,
        feed_gain_grad,
        gate_part,
        up_part,
        down_part,
    )


def solution(mesh):
    tokens = P("shard", ("context", "tensor"), None)
    rows = P("shard", None)
    weights = (P("shard"), rows, rows, rows, P("shard"), P("shard"), rows, P("shard")) + (
        P("shard", "tensor"),
        P("shard", "tensor"),
        P("tensor", "shard"),
    )
    placed = (tokens, tokens) + weights
    return jax.shard_map(
        on_device, mesh=mesh, in_specs=placed, out_specs=placed, check_vma=False
    )
```

```python
import jax
import jax.numpy as jnp
import numpy as np
from jax import lax
from jax.experimental import pallas as pl
from jax.experimental.pallas import tpu as pltpu
from jax.sharding import PartitionSpec as P

epsilon = 1e-05
rope_base = 1000000.0
masked_score = -1e30
line = ("context", "tensor")
f32 = jnp.float32
bf16 = jnp.bfloat16
piece = 128
half_head = 64
width = 1024
main = 512
packed = 3 * main + 256


def dot(a, b):
    return jnp.dot(a, b, preferred_element_type=f32)


def dot_nt(a, b):
    return lax.dot_general(a, b, (((1,), (1,)), ((), ())), preferred_element_type=f32)


def dot_tn(a, b):
    return lax.dot_general(a, b, (((0,), (0,)), ((), ())), preferred_element_type=f32)


def shape(dims, dtype):
    return jax.ShapeDtypeStruct(dims, dtype)


def estimate(micros):
    return pl.CostEstimate(flops=int(micros * 10**9), bytes_accessed=2**20, transcendentals=0)


room = {"attention_forward": 16, "attention_backward": 18, "feed_forward": 14, "pack": 60, "feed_pack": 60}


def big(value):
    return value.shape[0] > 1024


def call(body, outs, *args, micros=2, scratch=(), name=None, fetch=(), store=()):
    smem = pl.BlockSpec(memory_space=pltpu.SMEM)
    vmem = pl.BlockSpec(memory_space=pltpu.VMEM)
    anywhere = pl.BlockSpec(memory_space=pltpu.HBM)
    arrays = [i for i, a in enumerate(args) if a.dtype != jnp.int32]
    moved_in = arrays if fetch is True else list(fetch)
    moved_out = list(range(len(outs))) if store is True else list(store)
    buffers = [pltpu.VMEM(args[i].shape, args[i].dtype) for i in moved_in]
    buffers += [pltpu.VMEM(outs[i].shape, outs[i].dtype) for i in moved_out]
    count = len(buffers)
    if count:
        buffers.append(pltpu.SemaphoreType.DMA((count,)))

    def run(*refs):
        if not count:
            return body(*refs)
        refs = list(refs)
        first = len(args) + len(outs)
        held, sems = refs[first : first + count], refs[first + count]
        shown = refs[:first] + refs[first + count + 1 :]
        copies = []
        for slot, index in enumerate(moved_in):
            copy = pltpu.make_async_copy(refs[index], held[slot], sems.at[slot])
            copy.start()
            copies.append(copy)
            shown[index] = held[slot]
        for slot, index in enumerate(moved_out):
            shown[len(args) + index] = held[len(moved_in) + slot]
        for copy in copies:
            copy.wait()
        body(*shown)
        copies = []
        for slot, index in enumerate(moved_out):
            slot += len(moved_in)
            copy = pltpu.make_async_copy(held[slot], refs[len(args) + index], sems.at[slot])
            copy.start()
            copies.append(copy)
        for copy in copies:
            copy.wait()

    return pl.pallas_call(
        run,
        out_shape=tuple(outs),
        in_specs=[
            smem if i not in arrays else (anywhere if i in moved_in or big(args[i]) else vmem)
            for i in range(len(args))
        ],
        out_specs=tuple(anywhere if i in moved_out or big(o) else vmem for i, o in enumerate(outs)),
        scratch_shapes=buffers + list(scratch),
        compiler_params=pltpu.CompilerParams(vmem_limit_bytes=room.get(name, 12) * 2**20),
        cost_estimate=estimate(micros),
        name=name,
    )(*args)


def lanes(rows=1):
    return lax.broadcasted_iota(jnp.int32, (rows, piece), 1)


def mean_square_factor(value):
    return lax.rsqrt(jnp.mean(value * value, axis=-1, keepdims=True) + epsilon)


def halves_sum(value, low):
    first = jnp.sum(jnp.where(low, value, 0.0), axis=-1, keepdims=True)
    second = jnp.sum(jnp.where(low, 0.0, value), axis=-1, keepdims=True)
    return jnp.where(low, first, second)


def swapped_halves(value):
    return pltpu.roll(value, half_head, 1)


def turned(value, early):
    return jnp.where(early, pltpu.roll(value, 96, 1), pltpu.roll(value, 32, 1))


def place_of(me, core, chip):
    return me ^ (2 * chip + core)


def slot_of(me, place):
    partner = place ^ me
    return (partner % 2) * 4 + partner // 2


def feed_pack_kernel(info, gate, up, down, feed_out):
    context = info[2]
    low = lanes() < half_head
    late = context == 1
    start = pl.multiple_of(context * main, main)
    made = [ref[:, pl.ds(start, main)] for ref in (gate, up, down)]

    def rest(ref):
        tile = ref[:, 2 * main : 2 * main + piece].astype(f32)
        return jnp.where(late, swapped_halves(tile), tile)

    tail = jnp.where(low, rest(gate), swapped_halves(rest(up)))
    made.append(tail.astype(bf16))
    made.append(jnp.where(low, rest(down), 0.0).astype(bf16))
    block = jnp.concatenate(made, axis=1)
    for index in range(16):
        feed_out[index] = block


def pack_kernel(info, small, query, key, value, out, pack_out):
    shard, me = info[0], info[1]
    low = lanes() < half_head
    odd = me % 2 == 1

    def pair(ref):
        tile = ref[:, pl.ds(pl.multiple_of((me // 2) * piece, piece), piece)].astype(f32)
        return jnp.where(odd, swapped_halves(tile), tile)

    start = pl.multiple_of(me * piece, piece)
    keys = pair(key)
    values = swapped_halves(pair(value))
    pack = jnp.concatenate(
        [
            query[:, pl.ds(start, piece)],
            jnp.where(low, keys, values).astype(bf16),
            out[:, pl.ds(start, piece)],
        ],
        axis=1,
    )
    row = lax.broadcasted_iota(jnp.int32, (16, piece), 0)
    lane = lanes(16)
    ours = lane // half_head == shard % 2
    both = small[0:1, :]
    other = swapped_halves(both)
    gains = jnp.where(ours & (row == shard // 2), jnp.where(low, both, other), 0.0)
    gains = gains + jnp.where(ours & (row == 8 + shard // 2), jnp.where(low, other, both), 0.0)
    spot = (lane % half_head) // 4 == shard
    head_gains = jnp.zeros((16, piece), f32)
    for entry in range(4):
        here = spot & (lane % 4 == entry)
        query_gain = small[1:2, entry : entry + 1]
        key_gain = small[1:2, 4 + entry : 5 + entry]
        head_gains = head_gains + jnp.where(here & (row == 0), query_gain, 0.0)
        head_gains = head_gains + jnp.where(here & (row == 1), key_gain, 0.0)
    extra = jnp.concatenate([gains, head_gains, jnp.zeros((16, piece), f32)], axis=1)
    pack = jnp.concatenate([pack, extra.astype(bf16)], axis=0)
    for index in range(16):
        pack_out[index] = pack


def gathered_gains(pack):
    gains = pack[0, half_head:, :].astype(f32)
    for index in range(1, 16):
        gains = gains + pack[index, half_head:, :].astype(f32)
    return gains


def wide_gain(gains, first):
    return jnp.concatenate([gains[first + i : first + i + 1, :piece] for i in range(8)], axis=1)


def qkv_weight(pack):
    return pack[:, :half_head, : 2 * piece].reshape(width, 2 * piece)


def rounded(value):
    return value.astype(bf16).astype(f32)


def block_queries(ref, block, masks):
    both = ref[2 * block : 2 * block + 2].reshape(2 * piece, piece).astype(bf16)
    return jnp.concatenate([both * masks[0], both * masks[1]], axis=0)


def head_masks():
    low = (lanes() < half_head).astype(f32)
    return (low.astype(bf16), (1.0 - low).astype(bf16))


def block_scores(keys, stacked, count):
    score = dot_nt(keys, stacked) * (half_head**-0.5)
    span = 2 * piece
    row = lax.broadcasted_iota(jnp.int32, (span, 2 * span), 0)
    column = lax.broadcasted_iota(jnp.int32, (span, 2 * span), 1) % span
    own = jnp.where(row <= column, score[count - span :], masked_score)
    if count == span:
        return own
    return jnp.concatenate([score[: count - span], own], axis=0)


def pick_heads(wide):
    span = 2 * piece
    both = jnp.concatenate([wide[:half_head, :span], wide[half_head:, span:]], axis=0)
    return both.T


def angle_tables(table, place):
    start_cos, start_sin = table[pl.ds(place, 1), :], table[pl.ds(8 + place, 1), :]
    cos, sin = table[16 : 16 + piece, :], table[16 + piece :, :]
    return start_cos * cos - start_sin * sin, start_sin * cos + start_cos * sin


def forward_kernel(info, pack, mine, other, table, attended, mixer, log_out, gain_out, kept, raw, held, sem):
    me = info[1]
    query_out, key_out, value_out, query_normed, key_normed, query_factor, key_factor = [
        held.at[pl.ds(8 * i, 8)] for i in range(7)
    ]
    gains = gathered_gains(pack)
    gain_out[...] = gains
    gain = wide_gain(gains, 0)
    gain_query = gains[0:1, piece : 2 * piece]
    gain_key = gains[1:2, piece : 2 * piece]
    low = lanes() < half_head
    early = lanes() % half_head < half_head // 2
    for core, ref in enumerate((mine, other)):

        def prepare(chip, carry, ref=ref, core=core):
            x = ref[chip].astype(f32)
            mixer[core, chip] = (x * mean_square_factor(x) * gain).astype(bf16)
            return carry

        lax.fori_loop(0, 4, prepare, 0)
        raw[core] = dot(mixer[core].reshape(4 * piece, width), qkv_weight(pack)).reshape(
            4, piece, 2 * piece
        )

    def shape_heads(slot, carry):
        core, chip = slot // 4, slot % 4
        place = place_of(me, core, chip)
        block = raw[core, chip]
        query = block[:, :piece]
        both = block[:, piece:]
        other_way = swapped_halves(both)
        key = jnp.where(low, both, other_way)
        value_out[place] = rounded(jnp.where(low, other_way, both))
        factor = lax.rsqrt(halves_sum(query * query, low) / half_head + epsilon)
        normed = query * factor
        scaled = normed * gain_query
        cos, sin = angle_tables(table, place)
        sin = jnp.where(early, -sin, sin)
        query_out[place] = rounded(scaled * cos + turned(scaled, early) * sin)
        query_normed[place] = normed
        query_factor[place] = factor
        factor = jnp.broadcast_to(mean_square_factor(key), key.shape)
        normed = key * factor
        scaled = normed * gain_key
        key_out[place] = rounded(scaled * cos + turned(scaled, early) * sin)
        key_normed[place] = normed
        key_factor[place] = factor
        return carry

    lax.fori_loop(0, 8, shape_heads, 0)
    copy = pltpu.make_async_copy(held, kept.at[pl.ds(0, 56)], sem)
    copy.start()
    masks = head_masks()
    values_across = value_out[...].reshape(width, piece).T.astype(bf16)
    for block in range(4):
        count = 2 * piece * (block + 1)
        keys = key_out[: 2 * block + 2].reshape(count, piece).astype(bf16)
        score = block_scores(keys, block_queries(query_out, block, masks), count)
        peak = jnp.max(score, axis=0, keepdims=True)
        raised = jnp.exp(score - peak)
        total = jnp.sum(raised, axis=0, keepdims=True)
        chance = (raised * (1.0 / total)).astype(bf16)
        log_out[block] = peak + jnp.log(total)
        result = pick_heads(dot(values_across[:, :count], chance)).astype(bf16)
        for index in range(2):
            attended[slot_of(me, 2 * block + index)] = result[index * piece : (index + 1) * piece]
    copy.wait()


def branch_kernel(info, own, far, near, next_, mine, other, tokens, gains, mixed_out, feed_out, out_rows, attended):
    me = info[1]
    for chip, ref in enumerate((own, far, near, next_)):
        for core in range(2):
            start = pl.multiple_of(place_of(me, core, chip) * piece, piece)
            attended[:, pl.ds(start, piece)] = ref[core]
    rows = attended[...]
    own = pl.ds(pl.multiple_of(me * piece, piece), piece)
    for core, ref in enumerate((mine, other)):
        for chip in range(4):
            start = pl.multiple_of(place_of(me, core, chip) * piece, piece)
            mixed_out[:, pl.ds(start, piece)] = dot(rows, ref[chip])
            out_rows[:, pl.ds(start, piece)] = ref[chip, own, :]
    mixed = tokens[...].astype(f32) + mixed_out[...]
    mixed_out[...] = mixed
    gain = wide_gain(gains, 8)
    feed_out[...] = (mixed * mean_square_factor(mixed) * gain).astype(bf16)


def squash(value):
    return 1.0 / (1.0 + jnp.exp(-value))


def feed_kernel(feed_mine, feed_other, seed_mine, seed_other, weight, state, keep, give):
    low = lanes() < half_head

    def grads(gate, up, grad):
        squashed = squash(gate)
        activated = gate * squashed
        return (
            grad * up * squashed * (1.0 + gate * (1.0 - squashed)),
            grad * activated,
            activated * up,
        )

    starts = [0, main, 2 * main, 3 * main, 3 * main + piece, packed]

    def step(chip, carry):
        feed = jnp.concatenate([feed_mine[chip], feed_other[chip]], axis=0)
        seed = jnp.concatenate([seed_mine[chip], seed_other[chip]], axis=0)
        first = grads(
            dot(feed, weight[:, :main]),
            dot(feed, weight[:, main : 2 * main]),
            dot(seed, weight[:, 2 * main : 3 * main]),
        )
        pair = dot(feed, weight[:, 3 * main : 3 * main + piece])
        rest = grads(pair, swapped_halves(pair), dot(seed, weight[:, 3 * main + piece :]))
        made = [value.astype(bf16) for value in first]
        made.append(jnp.where(low, rest[0], swapped_halves(rest[1])).astype(bf16))
        made.append(jnp.where(low, rest[2], 0.0).astype(bf16))
        for index, value in enumerate(made):
            state[0, chip, :, starts[index] : starts[index + 1]] = value[:piece]
            state[1, chip, :, starts[index] : starts[index + 1]] = value[piece:]
        result = dot_nt(made[0], weight[:, :main]) + dot_nt(made[1], weight[:, main : 2 * main])
        result = result + dot_nt(made[3], weight[:, 3 * main : 3 * main + piece])
        result = result.astype(bf16)
        keep[chip] = result[:piece]
        give[chip] = result[piece:]
        return carry

    lax.fori_loop(0, 4, step, 0)


def feed_sums_kernel(feed_mine, feed_other, seed_mine, seed_other, state, sums):
    rows = 4 * piece

    def step(block, carry):
        columns = pl.ds(pl.multiple_of(block * 2 * piece, 2 * piece), 2 * piece)

        def both(mine, other, low, high):
            total = dot_tn(
                mine[:, :, columns].reshape(rows, 2 * piece),
                state[0, :, :, low:high].reshape(rows, high - low),
            )
            total = total + dot_tn(
                other[:, :, columns].reshape(rows, 2 * piece),
                state[1, :, :, low:high].reshape(rows, high - low),
            )
            sums[columns, low:high] = total.astype(bf16)

        both(feed_mine, feed_other, 0, 2 * main)
        both(seed_mine, seed_other, 2 * main, 3 * main)
        both(feed_mine, feed_other, 3 * main, 3 * main + piece)
        both(seed_mine, seed_other, 3 * main + piece, packed)
        return carry

    lax.fori_loop(0, 4, step, 0)


def feed_out_kernel(state, weight, keep, give):
    rows = 4 * piece
    for core, ref in ((1, give), (0, keep)):
        hidden = state[core, :, :, 2 * main : 3 * main].reshape(rows, main)
        result = dot_nt(hidden, weight[:, 2 * main : 3 * main])
        hidden = state[core, :, :, 3 * main + piece :].reshape(rows, piece)
        result = result + dot_nt(hidden, weight[:, 3 * main + piece :])
        ref[...] = result.astype(bf16).reshape(4, piece, width)


def meet_kernel(keep, got, own, far, near, next_):
    for chip, out in enumerate((own, far, near, next_)):
        out[...] = (keep[chip].astype(f32) + got[chip].astype(f32)).astype(bf16)


def grad_mixed_kernel(own, far, near, next_, mixed, seed, gains, grad_out, low_out):
    grad = own[...].astype(f32) + far[...].astype(f32) + near[...].astype(f32) + next_[...].astype(f32)
    x = mixed[...]
    factor = mean_square_factor(x)
    normed = x * factor
    scaled = grad * wide_gain(gains, 8)
    back = factor * (scaled - normed * jnp.mean(scaled * normed, axis=-1, keepdims=True))
    result = seed[...].astype(f32) + back
    grad_out[...] = result
    low_out[...] = result.astype(bf16)


def output_kernel(own, far, near, next_, mixed, out):
    total = own[...].astype(f32) + far[...].astype(f32) + near[...].astype(f32) + next_[...].astype(f32)
    out[...] = (mixed[...] + total).astype(bf16)


def input_kernel(own, far, near, next_, tokens, grad_mixed, gains, out):
    grad = own[...].astype(f32) + far[...].astype(f32) + near[...].astype(f32) + next_[...].astype(f32)
    x = tokens[...].astype(f32)
    factor = mean_square_factor(x)
    normed = x * factor
    scaled = grad * wide_gain(gains, 0)
    back = factor * (scaled - normed * jnp.mean(scaled * normed, axis=-1, keepdims=True))
    out[...] = (grad_mixed[...] + back).astype(bf16)


def backward_kernel(
    info, pack, gains, branch_mine, branch_other, out_rows, table, log_sum, kept,
    keep, give, raw_out, gain_out,
    grads, query_grad, key_grad, value_grad, held, sem,
):
    copy = pltpu.make_async_copy(kept.at[pl.ds(0, 56)], held, sem)
    copy.start()
    queries, keys, values, query_normed, key_normed, query_factor, key_factor = [
        held.at[pl.ds(8 * i, 8)] for i in range(7)
    ]
    me = info[1]
    low = lanes() < half_head
    early = lanes() % half_head < half_head // 2
    gain_query = gains[0:1, piece : 2 * piece]
    gain_key = gains[1:2, piece : 2 * piece]
    for core, ref in enumerate((branch_mine, branch_other)):
        grad = dot_nt(ref[...].reshape(4 * piece, width), out_rows[...]).astype(bf16)
        for chip in range(4):
            grads[place_of(me, core, chip)] = grad[chip * piece : (chip + 1) * piece]
    masks = head_masks()
    copy.wait()
    keys_across = keys[...].reshape(width, piece).T.astype(bf16)
    key_grad[...] = jnp.zeros_like(key_grad)
    value_grad[...] = jnp.zeros_like(value_grad)
    scale = half_head**-0.5
    for block in range(4):
        count = 2 * piece * (block + 1)
        some = 2 * block + 2
        key = keys[:some].reshape(count, piece).astype(bf16)
        value = values[:some].reshape(count, piece).astype(bf16)
        stacked = block_queries(queries, block, masks)
        grad = block_queries(grads, block, masks)
        chance = jnp.exp(block_scores(key, stacked, count) - log_sum[block])
        grad_chance = dot_nt(value, grad)
        inner = jnp.sum(chance * grad_chance, axis=0, keepdims=True)
        grad_score = (chance * (grad_chance - inner)).astype(bf16)
        value_grad[:some] += dot(chance.astype(bf16), grad).reshape(some, piece, piece)
        key_grad[:some] += dot(grad_score, stacked).reshape(some, piece, piece)
        result = pick_heads(dot(keys_across[:, :count], grad_score))
        query_grad[2 * block] = result[:piece]
        query_grad[2 * block + 1] = result[piece:]

    def finish(place, sums):
        cos, sin = angle_tables(table, place)
        sin = jnp.where(early, sin, -sin)

        def turn_back(value):
            return value * cos + turned(value, early) * sin

        grad = turn_back(rounded(query_grad[place] * scale))
        normed = query_normed[place]
        query_sum = sums[0] + jnp.sum(grad * normed, axis=0, keepdims=True)
        scaled = grad * gain_query
        mean = halves_sum(scaled * normed, low) / half_head
        raw_query = query_factor[place] * (scaled - normed * mean)
        both = key_grad[place]
        grad = turn_back(rounded((both + swapped_halves(both)) * scale))
        normed = key_normed[place]
        key_sum = sums[1] + jnp.sum(grad * normed, axis=0, keepdims=True)
        scaled = grad * gain_key
        mean = jnp.mean(scaled * normed, axis=-1, keepdims=True)
        raw_key = key_factor[place] * (scaled - normed * mean)
        both = value_grad[place]
        raw_value = both + swapped_halves(both)
        partner = place ^ me
        core, chip = partner % 2, partner // 2
        raw_out[core, chip, :, :piece] = raw_query.astype(bf16)
        raw_out[core, chip, :, piece:] = jnp.where(low, raw_key, raw_value).astype(bf16)
        return (query_sum, key_sum)

    zero = jnp.zeros((1, piece), f32)
    query_sum, key_sum = lax.fori_loop(0, 8, finish, (zero, zero))
    query_sum = query_sum + swapped_halves(query_sum)
    gain_out[...] = jnp.concatenate([query_sum, key_sum, jnp.zeros((6, piece), f32)], axis=0)
    for core, ref in ((1, give), (0, keep)):
        ref[...] = (
            dot_nt(raw_out[core].reshape(4 * piece, 2 * piece), qkv_weight(pack))
            .astype(bf16)
            .reshape(4, piece, width)
        )


def out_sums_kernel(info, attended, branch_mine, branch_other, sums):
    me = info[1]
    rows = 4 * piece
    total = dot_tn(attended[:4].reshape(rows, piece), branch_mine[...].reshape(rows, width))
    total = total + dot_tn(attended[4:].reshape(rows, piece), branch_other[...].reshape(rows, width))
    total = total.astype(bf16)
    for place in range(8):
        sums[slot_of(me, place)] = total[:, place * piece : (place + 1) * piece]


def pair_kernel(parts, got, own, far, near, next_):
    for chip, out in enumerate((own, far, near, next_)):
        out[0] = parts[chip]
        out[1] = got[chip]


def attention_sums_kernel(info, mixer, raw, own, far, near, next_, gain_sums, sums):
    total = dot_tn(mixer[...].reshape(width, width), raw[...].reshape(width, 2 * piece))
    sums[:, :half_head, : 2 * piece] = total.astype(bf16).reshape(16, half_head, 2 * piece)
    me = info[1]
    for chip, ref in enumerate((own, far, near, next_)):
        for core in range(2):
            place = place_of(me, core, chip)
            for index in range(2):
                block = ref[core, index * half_head : (index + 1) * half_head, :]
                sums[2 * place + index, :half_head, 2 * piece :] = block
    value = gain_sums[...]
    high = value.astype(bf16).astype(f32)
    tail = jnp.concatenate([high, value - high], axis=0)
    tail = jnp.concatenate([tail, jnp.zeros((16, 2 * piece), f32)], axis=1).astype(bf16)
    for index in range(16):
        sums[index, half_head:, :] = tail


def feed_total_kernel(parts, total, low):
    value = parts[0].astype(f32)
    for index in range(1, 16):
        value = value + parts[index].astype(f32)
    total[...] = value
    low[...] = value.astype(bf16)


def feed_outputs_kernel(info, own, other, gate, up, down):
    context = info[2]
    late = context == 1
    low = lanes() < half_head
    here = pl.multiple_of(context * main, main)
    there = pl.multiple_of((1 - context) * main, main)
    for index, ref in enumerate((gate, up, down)):
        span = slice(index * main, (index + 1) * main)
        ref[:, pl.ds(here, main)] = own[:, span].astype(f32)
        ref[:, pl.ds(there, main)] = other[:, span].astype(f32)
    span = slice(3 * main, 3 * main + piece)
    mine, far = own[:, span].astype(f32), other[:, span].astype(f32)
    first, second = jnp.where(late, far, mine), jnp.where(late, mine, far)
    gate[:, 2 * main :] = jnp.where(low, first, swapped_halves(second))
    up[:, 2 * main :] = jnp.where(low, swapped_halves(first), second)
    span = slice(3 * main + piece, packed)
    mine, far = own[:, span].astype(f32), other[:, span].astype(f32)
    first, second = jnp.where(late, far, mine), jnp.where(late, mine, far)
    down[:, 2 * main :] = jnp.where(low, first, swapped_halves(second))


def attention_total_kernel(parts, pack, feed_pack, feed_total, final):
    value = parts[0].astype(f32)
    for index in range(1, 16):
        value = value + parts[index].astype(f32)
    weights = value[:half_head]
    tail = value[half_head : half_head + 8, :piece] + value[half_head + 8 :, :piece]
    first = jnp.sum(
        pack[0, :half_head, : 2 * piece].astype(f32) * weights[:, : 2 * piece],
        axis=1,
        keepdims=True,
    )
    feed = jnp.sum(
        feed_pack[0, :, : 2 * main].astype(f32) * feed_total[:, : 2 * main].astype(f32), axis=1, keepdims=True
    )
    span = slice(3 * main, 3 * main + piece)
    feed = feed + jnp.sum(
        feed_pack[0, :, span].astype(f32) * feed_total[:, span].astype(f32), axis=1, keepdims=True
    )
    lane = lanes(half_head)
    spread = jnp.where(lane == 0, first, jnp.where(lane == 1, feed, 0.0))
    spread = jnp.concatenate([spread, jnp.zeros_like(spread)], axis=0).T
    rows = jnp.concatenate([spread[:8], tail], axis=0)
    rows = jnp.concatenate([rows, jnp.zeros((16, 2 * piece), f32)], axis=1)
    result = jnp.concatenate([weights, rows], axis=0).astype(bf16)
    for index in range(8):
        final[index] = result


def attention_outputs_kernel(small, final, query, key, value, out, gains):
    low = lanes() < half_head
    for place in range(8):
        span = slice(place * piece, (place + 1) * piece)
        query[:, span] = final[place, :half_head, :piece].astype(f32)
        out[:, span] = final[place, :half_head, 2 * piece :].astype(f32)
    for pair in range(4):
        span = slice(pair * piece, (pair + 1) * piece)
        first = final[2 * pair, :half_head, piece : 2 * piece].astype(f32)
        second = final[2 * pair + 1, :half_head, piece : 2 * piece].astype(f32)
        key[:, span] = jnp.where(low, first, swapped_halves(second))
        value[:, span] = jnp.where(low, swapped_halves(first), second)
    tail = final[0, half_head:, :piece].astype(f32)
    for place in range(1, 8):
        tail = tail + final[place, half_head:, :piece].astype(f32)
    both = small[0:1, :]
    gains[0:1] = tail[0:1] / both
    gains[1:2] = tail[1:2] / swapped_halves(both)
    gains[2:4] = tail[8:10]


def swap(value, bits):
    return lax.ppermute(value, line, [(i, i ^ bits) for i in range(8)])


def line_gather(block, *others):
    far, near, next_ = swap(block, 2), swap(block, 4), swap(block, 6)
    mine = jnp.stack([after(block, *others), far, near, next_])
    return mine, swap(mine, 1)


def line_reduce(keep, give, *others):
    got = swap(give, 1)
    keep = after(keep, *others)
    sent = call(meet_kernel, [shape((piece, width), bf16)] * 4, keep, got, micros=2, name="meet")
    return sent[0], swap(sent[1], 2), swap(sent[2], 4), swap(sent[3], 6)


def line_turn(parts):
    got = swap(parts[4:], 1)
    pair = shape((2,) + parts.shape[1:], parts.dtype)
    sent = call(pair_kernel, [pair] * 4, parts, got, micros=1, name="pair")
    return sent[0], swap(sent[1], 2), swap(sent[2], 4), swap(sent[3], 6)


def after(value, *others):
    return lax.optimization_barrier((value,) + others)[0]


def across(value):
    return lax.all_to_all(value, "shard", 0, 0, tiled=True)


def rope_table():
    frequency = rope_base ** (-np.arange(0, half_head, 2) / half_head)
    frequency = np.concatenate([frequency] * 4)[None, :]
    starts = np.arange(8)[:, None] * piece * frequency
    steps = np.arange(piece)[:, None] * frequency
    rows = [np.cos(starts), np.sin(starts), np.cos(steps), np.sin(steps)]
    return jnp.asarray(np.concatenate(rows), f32)


def on_device(
    tokens,
    cotangent,
    attention_gain,
    query_weight,
    key_weight,
    value_weight,
    query_gain,
    key_gain,
    out_weight,
    feed_gain,
    gate_weight,
    up_weight,
    down_weight,
):
    shard = lax.axis_index("shard")
    context = lax.axis_index("context")
    place = context * 4 + lax.axis_index("tensor")
    info = jnp.stack([shard, place, context]).astype(jnp.int32)
    token_rows = tokens.reshape(piece, width)
    seed_rows = cotangent.reshape(piece, width)
    small = jnp.concatenate(
        [attention_gain, feed_gain, query_gain, key_gain, jnp.zeros((120,), bf16)]
    )
    small = small.astype(f32).reshape(2, piece)
    (own_pack,) = call(
        pack_kernel,
        [shape((16, 80, 3 * piece), bf16)],
        info, small, query_weight, key_weight, value_weight, out_weight,
        micros=6,
        name="pack",
        fetch=True,
    )
    (feed_pack,) = call(
        feed_pack_kernel,
        [shape((16, half_head, packed), bf16)],
        info, gate_weight, up_weight, down_weight.T,
        micros=12,
        name="feed_pack",
        fetch=True,
    )
    pack = after(across(own_pack), feed_pack)
    feed_full = across(after(feed_pack, pack)).reshape(width, packed)
    out_columns = pack[:, :half_head, 2 * piece :].reshape(width, piece)
    tokens_mine, tokens_other = line_gather(token_rows, own_pack)
    seed_mine, seed_other = line_gather(after(seed_rows, tokens_mine))
    table = rope_table()
    cube = (8, piece, piece)
    attended_heads, mixer, log_sum, gains, kept = call(
        forward_kernel,
        [
            shape(cube, bf16), shape((2, 4, piece, width), bf16), shape((4, 1, 4 * piece), f32),
            shape((16, 3 * piece), f32), shape((1100, piece, piece), f32),
        ],
        info, pack, after(tokens_mine, seed_mine), tokens_other, table,
        micros=36,
        scratch=[
            pltpu.VMEM((2, 4, piece, 2 * piece), f32),
            pltpu.VMEM((56, piece, piece), f32),
            pltpu.SemaphoreType.DMA,
        ],
        name="attention_forward",
    )
    out_mine, out_other = line_gather(out_columns)
    attended = line_turn(attended_heads)
    mixed, feed_input, out_rows = call(
        branch_kernel,
        [shape((piece, width), f32), shape((piece, width), bf16), shape((piece, width), bf16)],
        info, *attended, out_mine, out_other, token_rows, gains,
        micros=2,
        scratch=[pltpu.VMEM((piece, width), bf16)],
        name="branch",
    )
    feed_mine, feed_other = line_gather(feed_input, feed_full)
    rows = (feed_mine, feed_other, seed_mine, seed_other)
    line_shape = shape((4, piece, width), bf16)
    state, grad_keep, grad_give = call(
        feed_kernel,
        [shape((2, 4, piece, packed), bf16), line_shape, line_shape],
        *rows, feed_full,
        micros=11,
        name="feed_forward",
    )
    grad_feed = line_reduce(grad_keep, grad_give)
    (sums,) = call(
        feed_sums_kernel,
        [shape((width, packed), bf16)],
        *rows, state,
        micros=8,
        name="feed_sums",
    )
    feed_parts = across(sums.reshape(16, half_head, packed))
    feed_total, feed_low = call(
        feed_total_kernel,
        [shape((half_head, packed), f32), shape((half_head, packed), bf16)],
        feed_parts,
        name="feed_total",
    )
    grad_mixed, grad_branch = call(
        grad_mixed_kernel,
        [shape((piece, width), f32), shape((piece, width), bf16)],
        after(grad_feed[0], sums), *grad_feed[1:], mixed, seed_rows, gains,
        name="grad_mixed",
    )
    (out_keep, out_give) = call(
        feed_out_kernel,
        [line_shape, line_shape],
        after(state, grad_branch), feed_full,
        micros=4,
        name="feed_out",
    )
    branch_mine, branch_other = line_gather(grad_branch, out_keep)
    (out_sums,) = call(
        out_sums_kernel,
        [shape(cube, bf16)],
        info, attended_heads, branch_mine, branch_other,
        micros=1,
        name="out_sums",
    )
    out_sums = line_turn(out_sums)
    cube_f32 = pltpu.VMEM(cube, f32)
    mixer_keep, mixer_give, raw, gain_sums = call(
        backward_kernel,
        [
            shape((4, piece, width), bf16),
            shape((4, piece, width), bf16),
            shape((2, 4, piece, 2 * piece), bf16),
            shape((8, piece), f32),
        ],
        info, pack, gains, branch_mine, branch_other, out_rows, table, log_sum, kept,
        micros=11,
        scratch=[
            pltpu.VMEM(cube, bf16), cube_f32, cube_f32, cube_f32,
            pltpu.VMEM((56, piece, piece), f32), pltpu.SemaphoreType.DMA,
        ],
        name="attention_backward",
    )
    (attention_sums,) = call(
        attention_sums_kernel,
        [shape((16, 80, 3 * piece), bf16)],
        info, after(mixer, feed_low), raw, *out_sums, gain_sums,
        micros=4,
        name="attention_sums",
    )
    grad_mixer = line_reduce(mixer_keep, mixer_give)
    attention_parts = across(after(attention_sums, grad_mixer[0]))
    (input_gradient,) = call(
        input_kernel,
        [shape((piece, width), bf16)],
        *grad_mixer, token_rows, grad_mixed, gains,
        name="input_gradient",
        store=True,
    )
    (output,) = call(
        output_kernel,
        [shape((piece, width), bf16)],
        *line_reduce(out_keep, after(out_give, raw)), mixed,
        name="output",
        store=True,
    )
    feed_far = swap(feed_low, 4)
    long = shape((half_head, 2 * main + piece), f32)
    gate_part, up_part, down_part = call(
        feed_outputs_kernel, [long, long, long], info, feed_total, feed_far, name="feed_outputs", store=True
    )
    (final,) = call(
        attention_total_kernel,
        [shape((8, 80, 3 * piece), bf16)],
        attention_parts, own_pack, feed_pack, feed_total,
        name="attention_total",
    )
    final = lax.all_to_all(final, line, 0, 0, tiled=True)
    query_part, key_part, value_part, out_part, gain_parts = call(
        attention_outputs_kernel,
        [
            shape((half_head, width), f32), shape((half_head, main), f32),
            shape((half_head, main), f32), shape((half_head, width), f32), shape((4, piece), f32),
        ],
        small, final,
        name="attention_outputs", store=True,
    )
    head_gains = lax.dynamic_slice(gain_parts, (2, 4 * shard), (2, 4))
    return (
        output.reshape(1, piece, width),
        input_gradient.reshape(1, piece, width),
        gain_parts[0, :half_head],
        query_part,
        key_part,
        value_part,
        head_gains[0],
        head_gains[1],
        out_part,
        gain_parts[1, :half_head],
        gate_part,
        up_part,
        down_part.T,
    )


def solution(mesh):
    tokens = P("shard", ("context", "tensor"), None)
    rows = P("shard", None)
    weights = (P("shard"), rows, rows, rows, P("shard"), P("shard"), rows, P("shard")) + (
        P("shard", "tensor"),
        P("shard", "tensor"),
        P("tensor", "shard"),
    )
    placed = (tokens, tokens) + weights
    return jax.shard_map(
        on_device, mesh=mesh, in_specs=placed, out_specs=placed, check_vma=False
    )
```

```python
import jax
import jax.numpy as jnp
import numpy as np
from jax import lax
from jax.experimental import pallas as pl
from jax.experimental.pallas import tpu as pltpu
from jax.sharding import PartitionSpec as P

epsilon = 1e-05
rope_base = 1000000.0
masked_score = -1e30
line = ("context", "tensor")
f32 = jnp.float32
bf16 = jnp.bfloat16
piece = 128
half_head = 64
width = 1024
main = 512
packed = 3 * main + 256


def dot(a, b):
    return jnp.dot(a, b, preferred_element_type=f32)


def dot_nt(a, b):
    return lax.dot_general(a, b, (((1,), (1,)), ((), ())), preferred_element_type=f32)


def dot_tn(a, b):
    return lax.dot_general(a, b, (((0,), (0,)), ((), ())), preferred_element_type=f32)


def shape(dims, dtype):
    return jax.ShapeDtypeStruct(dims, dtype)


def estimate(micros):
    return pl.CostEstimate(flops=int(micros * 10**9), bytes_accessed=2**20, transcendentals=0)


room = {"attention_forward": 16, "attention_backward": 18, "feed_forward": 14, "pack": 60, "feed_pack": 60}


def big(value):
    return value.shape[0] > 1024


def call(body, outs, *args, micros=2, scratch=(), name=None, fetch=(), store=()):
    smem = pl.BlockSpec(memory_space=pltpu.SMEM)
    vmem = pl.BlockSpec(memory_space=pltpu.VMEM)
    anywhere = pl.BlockSpec(memory_space=pltpu.HBM)
    arrays = [i for i, a in enumerate(args) if a.dtype != jnp.int32]
    moved_in = arrays if fetch is True else list(fetch)
    moved_out = list(range(len(outs))) if store is True else list(store)
    buffers = [pltpu.VMEM(args[i].shape, args[i].dtype) for i in moved_in]
    buffers += [pltpu.VMEM(outs[i].shape, outs[i].dtype) for i in moved_out]
    count = len(buffers)
    if count:
        buffers.append(pltpu.SemaphoreType.DMA((count,)))

    def run(*refs):
        if not count:
            return body(*refs)
        refs = list(refs)
        first = len(args) + len(outs)
        held, sems = refs[first : first + count], refs[first + count]
        shown = refs[:first] + refs[first + count + 1 :]
        copies = []
        for slot, index in enumerate(moved_in):
            copy = pltpu.make_async_copy(refs[index], held[slot], sems.at[slot])
            copy.start()
            copies.append(copy)
            shown[index] = held[slot]
        for slot, index in enumerate(moved_out):
            shown[len(args) + index] = held[len(moved_in) + slot]
        for copy in copies:
            copy.wait()
        body(*shown)
        copies = []
        for slot, index in enumerate(moved_out):
            slot += len(moved_in)
            copy = pltpu.make_async_copy(held[slot], refs[len(args) + index], sems.at[slot])
            copy.start()
            copies.append(copy)
        for copy in copies:
            copy.wait()

    return pl.pallas_call(
        run,
        out_shape=tuple(outs),
        in_specs=[
            smem if i not in arrays else (anywhere if i in moved_in or big(args[i]) else vmem)
            for i in range(len(args))
        ],
        out_specs=tuple(anywhere if i in moved_out or big(o) else vmem for i, o in enumerate(outs)),
        scratch_shapes=buffers + list(scratch),
        compiler_params=pltpu.CompilerParams(vmem_limit_bytes=room.get(name, 12) * 2**20),
        cost_estimate=estimate(micros),
        name=name,
    )(*args)


def lanes(rows=1):
    return lax.broadcasted_iota(jnp.int32, (rows, piece), 1)


def mean_square_factor(value):
    return lax.rsqrt(jnp.mean(value * value, axis=-1, keepdims=True) + epsilon)


def halves_sum(value, low):
    first = jnp.sum(jnp.where(low, value, 0.0), axis=-1, keepdims=True)
    second = jnp.sum(jnp.where(low, 0.0, value), axis=-1, keepdims=True)
    return jnp.where(low, first, second)


def swapped_halves(value):
    return pltpu.roll(value, half_head, 1)


def turned(value, early):
    return jnp.where(early, pltpu.roll(value, 96, 1), pltpu.roll(value, 32, 1))


def place_of(me, core, chip):
    return me ^ (2 * chip + core)


def slot_of(me, place):
    partner = place ^ me
    return (partner % 2) * 4 + partner // 2


def feed_pack_kernel(info, gate, up, down, feed_out, own_out):
    context = info[2]
    low = lanes() < half_head
    late = context == 1
    start = pl.multiple_of(context * main, main)
    made = [ref[:, pl.ds(start, main)] for ref in (gate, up, down)]

    def rest(ref):
        tile = ref[:, 2 * main : 2 * main + piece].astype(f32)
        return jnp.where(late, swapped_halves(tile), tile)

    tail = jnp.where(low, rest(gate), swapped_halves(rest(up)))
    made.append(tail.astype(bf16))
    made.append(jnp.where(low, rest(down), 0.0).astype(bf16))
    block = jnp.concatenate(made, axis=1)
    own_out[...] = block
    for index in range(16):
        feed_out[index] = block


def pack_kernel(
    info, first_gain, second_gain, query_gain, key_gain, query, key, value, out,
    pack_out, own_out, gain_out,
):
    shard, me = info[0], info[1]
    low = lanes() < half_head
    odd = me % 2 == 1

    def pair(ref):
        tile = ref[:, pl.ds(pl.multiple_of((me // 2) * piece, piece), piece)].astype(f32)
        return jnp.where(odd, swapped_halves(tile), tile)

    start = pl.multiple_of(me * piece, piece)
    keys = pair(key)
    values = swapped_halves(pair(value))
    pack = jnp.concatenate(
        [
            query[:, pl.ds(start, piece)],
            jnp.where(low, keys, values).astype(bf16),
            out[:, pl.ds(start, piece)],
        ],
        axis=1,
    )
    row = lax.broadcasted_iota(jnp.int32, (16, piece), 0)
    lane = lanes(16)
    ours = lane // half_head == shard % 2
    both = jnp.concatenate([first_gain[...], second_gain[...]], axis=1).astype(f32)
    gain_out[...] = jnp.broadcast_to(both, gain_out.shape)
    other = swapped_halves(both)
    gains = jnp.where(ours & (row == shard // 2), jnp.where(low, both, other), 0.0)
    gains = gains + jnp.where(ours & (row == 8 + shard // 2), jnp.where(low, other, both), 0.0)
    spot = (lane % half_head) // 4 == shard
    head_gains = jnp.zeros((16, piece), f32)
    for entry in range(4):
        here = spot & (lane % 4 == entry)
        value_query = query_gain[:, entry : entry + 1].astype(f32)
        value_key = key_gain[:, entry : entry + 1].astype(f32)
        head_gains = head_gains + jnp.where(here & (row == 0), value_query, 0.0)
        head_gains = head_gains + jnp.where(here & (row == 1), value_key, 0.0)
    own_out[...] = pack[:, : 2 * piece]
    extra = jnp.concatenate([gains, head_gains, jnp.zeros((16, piece), f32)], axis=1)
    pack = jnp.concatenate([pack, extra.astype(bf16)], axis=0)
    for index in range(16):
        pack_out[index] = pack


def gathered_gains(pack):
    gains = pack[0, half_head:, :].astype(f32)
    for index in range(1, 16):
        gains = gains + pack[index, half_head:, :].astype(f32)
    return gains


def wide_gain(gains, first):
    return jnp.concatenate([gains[first + i : first + i + 1, :piece] for i in range(8)], axis=1)


def qkv_weight(pack):
    return pack[:, :half_head, : 2 * piece].reshape(width, 2 * piece)


def rounded(value):
    return value.astype(bf16).astype(f32)


def block_queries(ref, block, masks):
    both = ref[2 * block : 2 * block + 2].reshape(2 * piece, piece).astype(bf16)
    return jnp.concatenate([both * masks[0], both * masks[1]], axis=0)


def head_masks():
    low = (lanes() < half_head).astype(f32)
    return (low.astype(bf16), (1.0 - low).astype(bf16))


def block_scores(keys, stacked, count):
    score = dot_nt(keys, stacked) * (half_head**-0.5)
    span = 2 * piece
    row = lax.broadcasted_iota(jnp.int32, (span, 2 * span), 0)
    column = lax.broadcasted_iota(jnp.int32, (span, 2 * span), 1) % span
    own = jnp.where(row <= column, score[count - span :], masked_score)
    if count == span:
        return own
    return jnp.concatenate([score[: count - span], own], axis=0)


def pick_heads(wide):
    span = 2 * piece
    both = jnp.concatenate([wide[:half_head, :span], wide[half_head:, span:]], axis=0)
    return both.T


def angle_tables(table, place):
    start_cos, start_sin = table[pl.ds(place, 1), :], table[pl.ds(8 + place, 1), :]
    cos, sin = table[16 : 16 + piece, :], table[16 + piece :, :]
    return start_cos * cos - start_sin * sin, start_sin * cos + start_cos * sin


def forward_kernel(info, pack, mine, other, table, attended, mixer, log_out, gain_out, kept, raw, held, sem):
    me = info[1]
    query_out, key_out, value_out, query_normed, key_normed, query_factor, key_factor = [
        held.at[pl.ds(8 * i, 8)] for i in range(7)
    ]
    gains = gathered_gains(pack)
    gain_out[...] = gains
    gain = wide_gain(gains, 0)
    gain_query = gains[0:1, piece : 2 * piece]
    gain_key = gains[1:2, piece : 2 * piece]
    low = lanes() < half_head
    early = lanes() % half_head < half_head // 2
    for core, ref in enumerate((mine, other)):

        def prepare(chip, carry, ref=ref, core=core):
            x = ref[chip].astype(f32)
            mixer[core, chip] = (x * mean_square_factor(x) * gain).astype(bf16)
            return carry

        lax.fori_loop(0, 4, prepare, 0)
        raw[core] = dot(mixer[core].reshape(4 * piece, width), qkv_weight(pack)).reshape(
            4, piece, 2 * piece
        )

    def shape_heads(slot, carry):
        core, chip = slot // 4, slot % 4
        place = place_of(me, core, chip)
        block = raw[core, chip]
        query = block[:, :piece]
        both = block[:, piece:]
        other_way = swapped_halves(both)
        key = jnp.where(low, both, other_way)
        value_out[place] = rounded(jnp.where(low, other_way, both))
        factor = lax.rsqrt(halves_sum(query * query, low) / half_head + epsilon)
        normed = query * factor
        scaled = normed * gain_query
        cos, sin = angle_tables(table, place)
        sin = jnp.where(early, -sin, sin)
        query_out[place] = rounded(scaled * cos + turned(scaled, early) * sin)
        query_normed[place] = normed
        query_factor[place] = factor
        factor = jnp.broadcast_to(mean_square_factor(key), key.shape)
        normed = key * factor
        scaled = normed * gain_key
        key_out[place] = rounded(scaled * cos + turned(scaled, early) * sin)
        key_normed[place] = normed
        key_factor[place] = factor
        return carry

    lax.fori_loop(0, 8, shape_heads, 0)
    copy = pltpu.make_async_copy(held, kept.at[pl.ds(0, 56)], sem)
    copy.start()
    masks = head_masks()
    values_across = value_out[...].reshape(width, piece).T.astype(bf16)
    for block in range(4):
        count = 2 * piece * (block + 1)
        keys = key_out[: 2 * block + 2].reshape(count, piece).astype(bf16)
        score = block_scores(keys, block_queries(query_out, block, masks), count)
        peak = jnp.max(score, axis=0, keepdims=True)
        raised = jnp.exp(score - peak)
        total = jnp.sum(raised, axis=0, keepdims=True)
        chance = (raised * (1.0 / total)).astype(bf16)
        log_out[block] = peak + jnp.log(total)
        result = pick_heads(dot(values_across[:, :count], chance)).astype(bf16)
        for index in range(2):
            attended[slot_of(me, 2 * block + index)] = result[index * piece : (index + 1) * piece]
    copy.wait()


def branch_kernel(info, own, far, near, next_, mine, other, tokens, gains, mixed_out, feed_out, out_rows, attended):
    me = info[1]
    for chip, ref in enumerate((own, far, near, next_)):
        for core in range(2):
            start = pl.multiple_of(place_of(me, core, chip) * piece, piece)
            attended[:, pl.ds(start, piece)] = ref[core]
    rows = attended[...]
    own = pl.ds(pl.multiple_of(me * piece, piece), piece)
    for core, ref in enumerate((mine, other)):
        for chip in range(4):
            start = pl.multiple_of(place_of(me, core, chip) * piece, piece)
            mixed_out[:, pl.ds(start, piece)] = dot(rows, ref[chip])
            out_rows[:, pl.ds(start, piece)] = ref[chip, own, :]
    mixed = tokens[...].astype(f32) + mixed_out[...]
    mixed_out[...] = mixed
    gain = wide_gain(gains, 8)
    feed_out[...] = (mixed * mean_square_factor(mixed) * gain).astype(bf16)


def squash(value):
    return 1.0 / (1.0 + jnp.exp(-value))


def feed_kernel(feed_mine, feed_other, seed_mine, seed_other, weight, state, keep, give):
    low = lanes() < half_head

    def grads(gate, up, grad):
        squashed = squash(gate)
        activated = gate * squashed
        return (
            grad * up * squashed * (1.0 + gate * (1.0 - squashed)),
            grad * activated,
            activated * up,
        )

    starts = [0, main, 2 * main, 3 * main, 3 * main + piece, packed]

    def step(chip, carry):
        feed = jnp.concatenate([feed_mine[chip], feed_other[chip]], axis=0)
        seed = jnp.concatenate([seed_mine[chip], seed_other[chip]], axis=0)
        first = grads(
            dot(feed, weight[:, :main]),
            dot(feed, weight[:, main : 2 * main]),
            dot(seed, weight[:, 2 * main : 3 * main]),
        )
        pair = dot(feed, weight[:, 3 * main : 3 * main + piece])
        rest = grads(pair, swapped_halves(pair), dot(seed, weight[:, 3 * main + piece :]))
        made = [value.astype(bf16) for value in first]
        made.append(jnp.where(low, rest[0], swapped_halves(rest[1])).astype(bf16))
        made.append(jnp.where(low, rest[2], 0.0).astype(bf16))
        for index, value in enumerate(made):
            state[0, chip, :, starts[index] : starts[index + 1]] = value[:piece]
            state[1, chip, :, starts[index] : starts[index + 1]] = value[piece:]
        result = dot_nt(made[0], weight[:, :main]) + dot_nt(made[1], weight[:, main : 2 * main])
        result = result + dot_nt(made[3], weight[:, 3 * main : 3 * main + piece])
        result = result.astype(bf16)
        keep[chip] = result[:piece]
        give[chip] = result[piece:]
        return carry

    lax.fori_loop(0, 4, step, 0)


def feed_sums_kernel(feed_mine, feed_other, seed_mine, seed_other, state, sums):
    rows = 4 * piece

    def step(block, carry):
        columns = pl.ds(pl.multiple_of(block * 2 * piece, 2 * piece), 2 * piece)

        def both(mine, other, low, high):
            total = dot_tn(
                mine[:, :, columns].reshape(rows, 2 * piece),
                state[0, :, :, low:high].reshape(rows, high - low),
            )
            total = total + dot_tn(
                other[:, :, columns].reshape(rows, 2 * piece),
                state[1, :, :, low:high].reshape(rows, high - low),
            )
            sums[columns, low:high] = total.astype(bf16)

        both(feed_mine, feed_other, 0, 2 * main)
        both(seed_mine, seed_other, 2 * main, 3 * main)
        both(feed_mine, feed_other, 3 * main, 3 * main + piece)
        both(seed_mine, seed_other, 3 * main + piece, packed)
        return carry

    lax.fori_loop(0, 4, step, 0)


def feed_out_kernel(state, weight, keep, give):
    rows = 4 * piece
    for core, ref in ((1, give), (0, keep)):
        hidden = state[core, :, :, 2 * main : 3 * main].reshape(rows, main)
        result = dot_nt(hidden, weight[:, 2 * main : 3 * main])
        hidden = state[core, :, :, 3 * main + piece :].reshape(rows, piece)
        result = result + dot_nt(hidden, weight[:, 3 * main + piece :])
        ref[...] = result.astype(bf16).reshape(4, piece, width)


def meet_kernel(keep, got, own, far, near, next_):
    for chip, out in enumerate((own, far, near, next_)):
        out[...] = (keep[chip].astype(f32) + got[chip].astype(f32)).astype(bf16)


def grad_mixed_kernel(own, far, near, next_, mixed, seed, gains, grad_out, low_out):
    grad = own[...].astype(f32) + far[...].astype(f32) + near[...].astype(f32) + next_[...].astype(f32)
    x = mixed[...]
    factor = mean_square_factor(x)
    normed = x * factor
    scaled = grad * wide_gain(gains, 8)
    back = factor * (scaled - normed * jnp.mean(scaled * normed, axis=-1, keepdims=True))
    result = seed[...].astype(f32) + back
    grad_out[...] = result
    low_out[...] = result.astype(bf16)


def output_kernel(own, far, near, next_, mixed, out):
    total = own[...].astype(f32) + far[...].astype(f32) + near[...].astype(f32) + next_[...].astype(f32)
    out[...] = (mixed[...] + total).astype(bf16)


def input_kernel(own, far, near, next_, tokens, grad_mixed, gains, out):
    grad = own[...].astype(f32) + far[...].astype(f32) + near[...].astype(f32) + next_[...].astype(f32)
    x = tokens[...].astype(f32)
    factor = mean_square_factor(x)
    normed = x * factor
    scaled = grad * wide_gain(gains, 0)
    back = factor * (scaled - normed * jnp.mean(scaled * normed, axis=-1, keepdims=True))
    out[...] = (grad_mixed[...] + back).astype(bf16)


def backward_kernel(
    info, pack, gains, branch_mine, branch_other, out_rows, table, log_sum, kept,
    keep, give, raw_out, gain_out,
    grads, query_grad, key_grad, value_grad, held, sem,
):
    copy = pltpu.make_async_copy(kept.at[pl.ds(0, 56)], held, sem)
    copy.start()
    queries, keys, values, query_normed, key_normed, query_factor, key_factor = [
        held.at[pl.ds(8 * i, 8)] for i in range(7)
    ]
    me = info[1]
    low = lanes() < half_head
    early = lanes() % half_head < half_head // 2
    gain_query = gains[0:1, piece : 2 * piece]
    gain_key = gains[1:2, piece : 2 * piece]
    for core, ref in enumerate((branch_mine, branch_other)):
        grad = dot_nt(ref[...].reshape(4 * piece, width), out_rows[...]).astype(bf16)
        for chip in range(4):
            grads[place_of(me, core, chip)] = grad[chip * piece : (chip + 1) * piece]
    masks = head_masks()
    copy.wait()
    keys_across = keys[...].reshape(width, piece).T.astype(bf16)
    key_grad[...] = jnp.zeros_like(key_grad)
    value_grad[...] = jnp.zeros_like(value_grad)
    scale = half_head**-0.5
    for block in range(4):
        count = 2 * piece * (block + 1)
        some = 2 * block + 2
        key = keys[:some].reshape(count, piece).astype(bf16)
        value = values[:some].reshape(count, piece).astype(bf16)
        stacked = block_queries(queries, block, masks)
        grad = block_queries(grads, block, masks)
        chance = jnp.exp(block_scores(key, stacked, count) - log_sum[block])
        grad_chance = dot_nt(value, grad)
        inner = jnp.sum(chance * grad_chance, axis=0, keepdims=True)
        grad_score = (chance * (grad_chance - inner)).astype(bf16)
        value_grad[:some] += dot(chance.astype(bf16), grad).reshape(some, piece, piece)
        key_grad[:some] += dot(grad_score, stacked).reshape(some, piece, piece)
        result = pick_heads(dot(keys_across[:, :count], grad_score))
        query_grad[2 * block] = result[:piece]
        query_grad[2 * block + 1] = result[piece:]

    def finish(place, sums):
        cos, sin = angle_tables(table, place)
        sin = jnp.where(early, sin, -sin)

        def turn_back(value):
            return value * cos + turned(value, early) * sin

        grad = turn_back(rounded(query_grad[place] * scale))
        normed = query_normed[place]
        query_sum = sums[0] + jnp.sum(grad * normed, axis=0, keepdims=True)
        scaled = grad * gain_query
        mean = halves_sum(scaled * normed, low) / half_head
        raw_query = query_factor[place] * (scaled - normed * mean)
        both = key_grad[place]
        grad = turn_back(rounded((both + swapped_halves(both)) * scale))
        normed = key_normed[place]
        key_sum = sums[1] + jnp.sum(grad * normed, axis=0, keepdims=True)
        scaled = grad * gain_key
        mean = jnp.mean(scaled * normed, axis=-1, keepdims=True)
        raw_key = key_factor[place] * (scaled - normed * mean)
        both = value_grad[place]
        raw_value = both + swapped_halves(both)
        partner = place ^ me
        core, chip = partner % 2, partner // 2
        raw_out[core, chip, :, :piece] = raw_query.astype(bf16)
        raw_out[core, chip, :, piece:] = jnp.where(low, raw_key, raw_value).astype(bf16)
        return (query_sum, key_sum)

    zero = jnp.zeros((1, piece), f32)
    query_sum, key_sum = lax.fori_loop(0, 8, finish, (zero, zero))
    query_sum = query_sum + swapped_halves(query_sum)
    gain_out[...] = jnp.concatenate([query_sum, key_sum, jnp.zeros((6, piece), f32)], axis=0)
    for core, ref in ((1, give), (0, keep)):
        ref[...] = (
            dot_nt(raw_out[core].reshape(4 * piece, 2 * piece), qkv_weight(pack))
            .astype(bf16)
            .reshape(4, piece, width)
        )


def out_sums_kernel(info, attended, branch_mine, branch_other, sums):
    me = info[1]
    rows = 4 * piece
    total = dot_tn(attended[:4].reshape(rows, piece), branch_mine[...].reshape(rows, width))
    total = total + dot_tn(attended[4:].reshape(rows, piece), branch_other[...].reshape(rows, width))
    total = total.astype(bf16)
    for place in range(8):
        sums[slot_of(me, place)] = total[:, place * piece : (place + 1) * piece]


def pair_kernel(parts, got, own, far, near, next_):
    for chip, out in enumerate((own, far, near, next_)):
        out[0] = parts[chip]
        out[1] = got[chip]


def attention_sums_kernel(info, mixer, raw, own, far, near, next_, gain_sums, sums):
    total = dot_tn(mixer[...].reshape(width, width), raw[...].reshape(width, 2 * piece))
    sums[:, :half_head, : 2 * piece] = total.astype(bf16).reshape(16, half_head, 2 * piece)
    me = info[1]
    for chip, ref in enumerate((own, far, near, next_)):
        for core in range(2):
            place = place_of(me, core, chip)
            for index in range(2):
                block = ref[core, index * half_head : (index + 1) * half_head, :]
                sums[2 * place + index, :half_head, 2 * piece :] = block
    value = gain_sums[...]
    high = value.astype(bf16).astype(f32)
    tail = jnp.concatenate([high, value - high], axis=0)
    tail = jnp.concatenate([tail, jnp.zeros((16, 2 * piece), f32)], axis=1).astype(bf16)
    for index in range(16):
        sums[index, half_head:, :] = tail


def feed_total_kernel(parts, total, low):
    value = parts[0].astype(f32)
    for index in range(1, 16):
        value = value + parts[index].astype(f32)
    total[...] = value
    low[...] = value.astype(bf16)


def feed_outputs_kernel(info, own, other, gate, up, down):
    context = info[2]
    late = context == 1
    low = lanes() < half_head
    here = pl.multiple_of(context * main, main)
    there = pl.multiple_of((1 - context) * main, main)
    for index, ref in enumerate((gate, up, down)):
        span = slice(index * main, (index + 1) * main)
        ref[:, pl.ds(here, main)] = own[:, span].astype(f32)
        ref[:, pl.ds(there, main)] = other[:, span].astype(f32)
    span = slice(3 * main, 3 * main + piece)
    mine, far = own[:, span].astype(f32), other[:, span].astype(f32)
    first, second = jnp.where(late, far, mine), jnp.where(late, mine, far)
    gate[:, 2 * main :] = jnp.where(low, first, swapped_halves(second))
    up[:, 2 * main :] = jnp.where(low, swapped_halves(first), second)
    span = slice(3 * main + piece, packed)
    mine, far = own[:, span].astype(f32), other[:, span].astype(f32)
    first, second = jnp.where(late, far, mine), jnp.where(late, mine, far)
    down[:, 2 * main :] = jnp.where(low, first, swapped_halves(second))


def attention_total_kernel(parts, pack, feed_pack, feed_total, final):
    value = parts[0].astype(f32)
    for index in range(1, 16):
        value = value + parts[index].astype(f32)
    weights = value[:half_head]
    tail = value[half_head : half_head + 8, :piece] + value[half_head + 8 :, :piece]
    first = jnp.sum(
        pack[...].astype(f32) * weights[:, : 2 * piece],
        axis=1,
        keepdims=True,
    )
    feed = jnp.sum(
        feed_pack[:, : 2 * main].astype(f32) * feed_total[:, : 2 * main].astype(f32), axis=1, keepdims=True
    )
    span = slice(3 * main, 3 * main + piece)
    feed = feed + jnp.sum(
        feed_pack[:, span].astype(f32) * feed_total[:, span].astype(f32), axis=1, keepdims=True
    )
    lane = lanes(half_head)
    spread = jnp.where(lane == 0, first, jnp.where(lane == 1, feed, 0.0))
    spread = jnp.concatenate([spread, jnp.zeros_like(spread)], axis=0).T
    rows = jnp.concatenate([spread[:8], tail], axis=0)
    rows = jnp.concatenate([rows, jnp.zeros((16, 2 * piece), f32)], axis=1)
    result = jnp.concatenate([weights, rows], axis=0).astype(bf16)
    for index in range(8):
        final[index] = result


def attention_outputs_kernel(small, final, query, key, value, out, gains):
    low = lanes() < half_head
    for place in range(8):
        span = slice(place * piece, (place + 1) * piece)
        query[:, span] = final[place, :half_head, :piece].astype(f32)
        out[:, span] = final[place, :half_head, 2 * piece :].astype(f32)
    for pair in range(4):
        span = slice(pair * piece, (pair + 1) * piece)
        first = final[2 * pair, :half_head, piece : 2 * piece].astype(f32)
        second = final[2 * pair + 1, :half_head, piece : 2 * piece].astype(f32)
        key[:, span] = jnp.where(low, first, swapped_halves(second))
        value[:, span] = jnp.where(low, swapped_halves(first), second)
    tail = final[0, half_head:, :piece].astype(f32)
    for place in range(1, 8):
        tail = tail + final[place, half_head:, :piece].astype(f32)
    both = small[0:1, :]
    gains[0:1] = tail[0:1] / both
    gains[1:2] = tail[1:2] / swapped_halves(both)
    gains[2:4] = tail[8:10]


def swap(value, bits):
    return lax.ppermute(value, line, [(i, i ^ bits) for i in range(8)])


def line_gather(block, *others):
    far, near, next_ = swap(block, 2), swap(block, 4), swap(block, 6)
    mine = jnp.stack([after(block, *others), far, near, next_])
    return mine, swap(mine, 1)


def line_reduce(keep, give, *others):
    got = swap(give, 1)
    keep = after(keep, *others)
    sent = call(meet_kernel, [shape((piece, width), bf16)] * 4, keep, got, micros=2, name="meet")
    return sent[0], swap(sent[1], 2), swap(sent[2], 4), swap(sent[3], 6)


def line_turn(parts):
    got = swap(parts[4:], 1)
    pair = shape((2,) + parts.shape[1:], parts.dtype)
    sent = call(pair_kernel, [pair] * 4, parts, got, micros=1, name="pair")
    return sent[0], swap(sent[1], 2), swap(sent[2], 4), swap(sent[3], 6)


def after(value, *others):
    return lax.optimization_barrier((value,) + others)[0]


def across(value):
    return lax.all_to_all(value, "shard", 0, 0, tiled=True)


def rope_table():
    frequency = rope_base ** (-np.arange(0, half_head, 2) / half_head)
    frequency = np.concatenate([frequency] * 4)[None, :]
    starts = np.arange(8)[:, None] * piece * frequency
    steps = np.arange(piece)[:, None] * frequency
    rows = [np.cos(starts), np.sin(starts), np.cos(steps), np.sin(steps)]
    return jnp.asarray(np.concatenate(rows), f32)


def on_device(
    tokens,
    cotangent,
    attention_gain,
    query_weight,
    key_weight,
    value_weight,
    query_gain,
    key_gain,
    out_weight,
    feed_gain,
    gate_weight,
    up_weight,
    down_weight,
):
    shard = lax.axis_index("shard")
    context = lax.axis_index("context")
    place = context * 4 + lax.axis_index("tensor")
    info = jnp.stack([shard, place, context]).astype(jnp.int32)
    token_rows = tokens.reshape(piece, width)
    seed_rows = cotangent.reshape(piece, width)
    gains = [value.reshape(1, -1) for value in (attention_gain, feed_gain, query_gain, key_gain)]
    pack, own_pack, small = call(
        pack_kernel,
        [
            shape((16, 80, 3 * piece), bf16),
            shape((half_head, 2 * piece), bf16),
            shape((8, piece), f32),
        ],
        info, *gains, query_weight, key_weight, value_weight, out_weight,
        micros=6,
        name="pack",
        fetch=True,
    )
    feed_pack, own_feed = call(
        feed_pack_kernel,
        [shape((16, half_head, packed), bf16), shape((half_head, packed), bf16)],
        info, gate_weight, up_weight, down_weight.T,
        micros=12,
        name="feed_pack",
        fetch=True,
    )
    pack = after(across(pack), feed_pack)
    feed_full = across(after(feed_pack, pack)).reshape(width, packed)
    out_columns = pack[:, :half_head, 2 * piece :].reshape(width, piece)
    tokens_mine, tokens_other = line_gather(token_rows, own_pack)
    seed_mine, seed_other = line_gather(after(seed_rows, tokens_mine))
    table = rope_table()
    cube = (8, piece, piece)
    attended_heads, mixer, log_sum, gains, kept = call(
        forward_kernel,
        [
            shape(cube, bf16), shape((2, 4, piece, width), bf16), shape((4, 1, 4 * piece), f32),
            shape((16, 3 * piece), f32), shape((1100, piece, piece), f32),
        ],
        info, pack, after(tokens_mine, seed_mine), tokens_other, table,
        micros=36,
        scratch=[
            pltpu.VMEM((2, 4, piece, 2 * piece), f32),
            pltpu.VMEM((56, piece, piece), f32),
            pltpu.SemaphoreType.DMA,
        ],
        name="attention_forward",
    )
    out_mine, out_other = line_gather(out_columns, attended_heads)
    attended = line_turn(attended_heads)
    mixed, feed_input, out_rows = call(
        branch_kernel,
        [shape((piece, width), f32), shape((piece, width), bf16), shape((piece, width), bf16)],
        info, *attended, out_mine, out_other, token_rows, gains,
        micros=2,
        scratch=[pltpu.VMEM((piece, width), bf16)],
        name="branch",
    )
    feed_mine, feed_other = line_gather(feed_input, feed_full)
    rows = (feed_mine, feed_other, seed_mine, seed_other)
    line_shape = shape((4, piece, width), bf16)
    state, grad_keep, grad_give = call(
        feed_kernel,
        [shape((2, 4, piece, packed), bf16), line_shape, line_shape],
        *rows, feed_full,
        micros=11,
        name="feed_forward",
    )
    grad_feed = line_reduce(grad_keep, grad_give)
    (sums,) = call(
        feed_sums_kernel,
        [shape((width, packed), bf16)],
        *rows, state,
        micros=8,
        name="feed_sums",
    )
    feed_parts = across(sums.reshape(16, half_head, packed))
    grad_mixed, grad_branch = call(
        grad_mixed_kernel,
        [shape((piece, width), f32), shape((piece, width), bf16)],
        after(grad_feed[0], sums), *grad_feed[1:], mixed, seed_rows, gains,
        name="grad_mixed",
    )
    (out_keep, out_give) = call(
        feed_out_kernel,
        [line_shape, line_shape],
        after(state, grad_branch), feed_full,
        micros=4,
        name="feed_out",
    )
    branch_mine, branch_other = line_gather(grad_branch, out_keep)
    (out_parts,) = call(
        out_sums_kernel,
        [shape(cube, bf16)],
        info, attended_heads, branch_mine, branch_other,
        micros=1,
        name="out_sums",
    )
    out_sums = line_turn(out_parts)
    cube_f32 = pltpu.VMEM(cube, f32)
    mixer_keep, mixer_give, raw, gain_sums = call(
        backward_kernel,
        [
            shape((4, piece, width), bf16),
            shape((4, piece, width), bf16),
            shape((2, 4, piece, 2 * piece), bf16),
            shape((8, piece), f32),
        ],
        info, pack, gains, branch_mine, branch_other, after(out_rows, out_parts), table, log_sum, kept,
        micros=6,
        scratch=[
            pltpu.VMEM(cube, bf16), cube_f32, cube_f32, cube_f32,
            pltpu.VMEM((56, piece, piece), f32), pltpu.SemaphoreType.DMA,
        ],
        name="attention_backward",
    )
    (attention_sums,) = call(
        attention_sums_kernel,
        [shape((16, 80, 3 * piece), bf16)],
        info, mixer, raw, *out_sums, gain_sums,
        micros=2,
        name="attention_sums",
    )
    grad_mixer = line_reduce(mixer_keep, mixer_give)
    attention_parts = across(after(attention_sums, *grad_mixer[1:]))
    feed_total, feed_low = call(
        feed_total_kernel,
        [shape((half_head, packed), f32), shape((half_head, packed), bf16)],
        after(feed_parts, attention_sums),
        name="feed_total",
    )
    (input_gradient,) = call(
        input_kernel,
        [shape((piece, width), bf16)],
        *grad_mixer, token_rows, grad_mixed, gains,
        name="input_gradient",
        store=True,
    )
    (output,) = call(
        output_kernel,
        [shape((piece, width), bf16)],
        *line_reduce(out_keep, after(out_give, raw)), mixed,
        name="output",
        store=True,
    )
    feed_far = swap(feed_low, 4)
    long = shape((half_head, 2 * main + piece), f32)
    gate_part, up_part, down_part = call(
        feed_outputs_kernel, [long, long, long], info, feed_total, feed_far, name="feed_outputs", store=True
    )
    (final,) = call(
        attention_total_kernel,
        [shape((8, 80, 3 * piece), bf16)],
        attention_parts, own_pack, own_feed, feed_total,
        name="attention_total",
    )
    final = lax.all_to_all(final, line, 0, 0, tiled=True)
    query_part, key_part, value_part, out_part, gain_parts = call(
        attention_outputs_kernel,
        [
            shape((half_head, width), f32), shape((half_head, main), f32),
            shape((half_head, main), f32), shape((half_head, width), f32), shape((4, piece), f32),
        ],
        small, final,
        name="attention_outputs", store=True,
    )
    head_gains = lax.dynamic_slice(gain_parts, (2, 4 * shard), (2, 4))
    return (
        output.reshape(1, piece, width),
        input_gradient.reshape(1, piece, width),
        gain_parts[0, :half_head],
        query_part,
        key_part,
        value_part,
        head_gains[0],
        head_gains[1],
        out_part,
        gain_parts[1, :half_head],
        gate_part,
        up_part,
        down_part.T,
    )


def solution(mesh):
    tokens = P("shard", ("context", "tensor"), None)
    rows = P("shard", None)
    weights = (P("shard"), rows, rows, rows, P("shard"), P("shard"), rows, P("shard")) + (
        P("shard", "tensor"),
        P("shard", "tensor"),
        P("tensor", "shard"),
    )
    placed = (tokens, tokens) + weights
    return jax.shard_map(
        on_device, mesh=mesh, in_specs=placed, out_specs=placed, check_vma=False
    )
```

```python
import jax
import jax.numpy as jnp
import numpy as np
from jax import lax
from jax.experimental import pallas as pl
from jax.experimental.pallas import tpu as pltpu
from jax.sharding import PartitionSpec as P

epsilon = 1e-05
rope_base = 1000000.0
masked_score = -1e30
line = ("context", "tensor")
f32 = jnp.float32
bf16 = jnp.bfloat16
piece = 128
half_head = 64
width = 1024
main = 512
packed = 3 * main + 256


def dot(a, b):
    return jnp.dot(a, b, preferred_element_type=f32)


def dot_nt(a, b):
    return lax.dot_general(a, b, (((1,), (1,)), ((), ())), preferred_element_type=f32)


def dot_tn(a, b):
    return lax.dot_general(a, b, (((0,), (0,)), ((), ())), preferred_element_type=f32)


def shape(dims, dtype):
    return jax.ShapeDtypeStruct(dims, dtype)


def estimate(micros):
    return pl.CostEstimate(flops=int(micros * 10**9), bytes_accessed=2**20, transcendentals=0)


room = {"attention_forward": 16, "attention_backward": 18, "feed_forward": 14, "pack": 60, "feed_pack": 60}


def big(value):
    return value.shape[0] > 1024


def call(body, outs, *args, micros=2, scratch=(), name=None, fetch=(), store=()):
    smem = pl.BlockSpec(memory_space=pltpu.SMEM)
    vmem = pl.BlockSpec(memory_space=pltpu.VMEM)
    anywhere = pl.BlockSpec(memory_space=pltpu.HBM)
    arrays = [i for i, a in enumerate(args) if a.dtype != jnp.int32]
    moved_in = arrays if fetch is True else list(fetch)
    moved_out = list(range(len(outs))) if store is True else list(store)
    buffers = [pltpu.VMEM(args[i].shape, args[i].dtype) for i in moved_in]
    buffers += [pltpu.VMEM(outs[i].shape, outs[i].dtype) for i in moved_out]
    count = len(buffers)
    if count:
        buffers.append(pltpu.SemaphoreType.DMA((count,)))

    def run(*refs):
        if not count:
            return body(*refs)
        refs = list(refs)
        first = len(args) + len(outs)
        held, sems = refs[first : first + count], refs[first + count]
        shown = refs[:first] + refs[first + count + 1 :]
        copies = []
        for slot, index in enumerate(moved_in):
            copy = pltpu.make_async_copy(refs[index], held[slot], sems.at[slot])
            copy.start()
            copies.append(copy)
            shown[index] = held[slot]
        for slot, index in enumerate(moved_out):
            shown[len(args) + index] = held[len(moved_in) + slot]
        for copy in copies:
            copy.wait()
        body(*shown)
        copies = []
        for slot, index in enumerate(moved_out):
            slot += len(moved_in)
            copy = pltpu.make_async_copy(held[slot], refs[len(args) + index], sems.at[slot])
            copy.start()
            copies.append(copy)
        for copy in copies:
            copy.wait()

    return pl.pallas_call(
        run,
        out_shape=tuple(outs),
        in_specs=[
            smem if i not in arrays else (anywhere if i in moved_in or big(args[i]) else vmem)
            for i in range(len(args))
        ],
        out_specs=tuple(anywhere if i in moved_out or big(o) else vmem for i, o in enumerate(outs)),
        scratch_shapes=buffers + list(scratch),
        compiler_params=pltpu.CompilerParams(vmem_limit_bytes=room.get(name, 12) * 2**20),
        cost_estimate=estimate(micros),
        name=name,
    )(*args)


def lanes(rows=1):
    return lax.broadcasted_iota(jnp.int32, (rows, piece), 1)


def mean_square_factor(value):
    return lax.rsqrt(jnp.mean(value * value, axis=-1, keepdims=True) + epsilon)


def halves_sum(value, low):
    first = jnp.sum(jnp.where(low, value, 0.0), axis=-1, keepdims=True)
    second = jnp.sum(jnp.where(low, 0.0, value), axis=-1, keepdims=True)
    return jnp.where(low, first, second)


def swapped_halves(value):
    return pltpu.roll(value, half_head, 1)


def turned(value, early):
    return jnp.where(early, pltpu.roll(value, 96, 1), pltpu.roll(value, 32, 1))


def place_of(me, core, chip):
    return me ^ (2 * chip + core)


def slot_of(me, place):
    partner = place ^ me
    return (partner % 2) * 4 + partner // 2


def feed_pack_kernel(info, gate, up, down, feed_out, own_out):
    context = info[2]
    low = lanes() < half_head
    late = context == 1
    start = pl.multiple_of(context * main, main)
    made = [ref[:, pl.ds(start, main)] for ref in (gate, up, down)]

    def rest(ref):
        tile = ref[:, 2 * main : 2 * main + piece].astype(f32)
        return jnp.where(late, swapped_halves(tile), tile)

    tail = jnp.where(low, rest(gate), swapped_halves(rest(up)))
    made.append(tail.astype(bf16))
    made.append(jnp.where(low, rest(down), 0.0).astype(bf16))
    block = jnp.concatenate(made, axis=1)
    own_out[...] = block
    for index in range(16):
        feed_out[index] = block


def pack_kernel(
    info, first_gain, second_gain, query_gain, key_gain, query, key, value, out,
    pack_out, own_out, gain_out,
):
    shard, me = info[0], info[1]
    low = lanes() < half_head
    odd = me % 2 == 1

    def pair(ref):
        tile = ref[:, pl.ds(pl.multiple_of((me // 2) * piece, piece), piece)].astype(f32)
        return jnp.where(odd, swapped_halves(tile), tile)

    start = pl.multiple_of(me * piece, piece)
    keys = pair(key)
    values = swapped_halves(pair(value))
    pack = jnp.concatenate(
        [
            query[:, pl.ds(start, piece)],
            jnp.where(low, keys, values).astype(bf16),
            out[:, pl.ds(start, piece)],
        ],
        axis=1,
    )
    row = lax.broadcasted_iota(jnp.int32, (16, piece), 0)
    lane = lanes(16)
    ours = lane // half_head == shard % 2
    both = jnp.concatenate([first_gain[...], second_gain[...]], axis=1).astype(f32)
    gain_out[...] = jnp.broadcast_to(both, gain_out.shape)
    other = swapped_halves(both)
    gains = jnp.where(ours & (row == shard // 2), jnp.where(low, both, other), 0.0)
    gains = gains + jnp.where(ours & (row == 8 + shard // 2), jnp.where(low, other, both), 0.0)
    spot = (lane % half_head) // 4 == shard
    head_gains = jnp.zeros((16, piece), f32)
    for entry in range(4):
        here = spot & (lane % 4 == entry)
        value_query = query_gain[:, entry : entry + 1].astype(f32)
        value_key = key_gain[:, entry : entry + 1].astype(f32)
        head_gains = head_gains + jnp.where(here & (row == 0), value_query, 0.0)
        head_gains = head_gains + jnp.where(here & (row == 1), value_key, 0.0)
    own_out[...] = pack[:, : 2 * piece]
    extra = jnp.concatenate([gains, head_gains, jnp.zeros((16, piece), f32)], axis=1)
    pack = jnp.concatenate([pack, extra.astype(bf16)], axis=0)
    for index in range(16):
        pack_out[index] = pack


def gathered_gains(pack):
    gains = pack[0, half_head:, :].astype(f32)
    for index in range(1, 16):
        gains = gains + pack[index, half_head:, :].astype(f32)
    return gains


def wide_gain(gains, first):
    return jnp.concatenate([gains[first + i : first + i + 1, :piece] for i in range(8)], axis=1)


def qkv_weight(pack):
    return pack[:, :half_head, : 2 * piece].reshape(width, 2 * piece)


def rounded(value):
    return value.astype(bf16).astype(f32)


def block_queries(ref, block, masks):
    both = ref[2 * block : 2 * block + 2].reshape(2 * piece, piece).astype(bf16)
    return jnp.concatenate([both * masks[0], both * masks[1]], axis=0)


def head_masks():
    low = (lanes() < half_head).astype(f32)
    return (low.astype(bf16), (1.0 - low).astype(bf16))


def block_scores(keys, stacked, count):
    score = dot_nt(keys, stacked) * (half_head**-0.5)
    span = 2 * piece
    row = lax.broadcasted_iota(jnp.int32, (span, 2 * span), 0)
    column = lax.broadcasted_iota(jnp.int32, (span, 2 * span), 1) % span
    own = jnp.where(row <= column, score[count - span :], masked_score)
    if count == span:
        return own
    return jnp.concatenate([score[: count - span], own], axis=0)


def pick_heads(wide):
    span = 2 * piece
    both = jnp.concatenate([wide[:half_head, :span], wide[half_head:, span:]], axis=0)
    return both.T


def angle_tables(table, place):
    start_cos, start_sin = table[pl.ds(place, 1), :], table[pl.ds(8 + place, 1), :]
    cos, sin = table[16 : 16 + piece, :], table[16 + piece :, :]
    return start_cos * cos - start_sin * sin, start_sin * cos + start_cos * sin


def forward_kernel(info, pack, mine, other, table, attended, mixer, log_out, gain_out, kept, raw, held, sem):
    me = info[1]
    query_out, key_out, value_out, query_normed, key_normed, query_factor, key_factor = [
        held.at[pl.ds(8 * i, 8)] for i in range(7)
    ]
    gains = gathered_gains(pack)
    gain_out[...] = gains
    gain = wide_gain(gains, 0)
    gain_query = gains[0:1, piece : 2 * piece]
    gain_key = gains[1:2, piece : 2 * piece]
    low = lanes() < half_head
    early = lanes() % half_head < half_head // 2
    for core, ref in enumerate((mine, other)):

        def prepare(chip, carry, ref=ref, core=core):
            x = ref[chip].astype(f32)
            mixer[core, chip] = (x * mean_square_factor(x) * gain).astype(bf16)
            return carry

        lax.fori_loop(0, 4, prepare, 0)
        raw[core] = dot(mixer[core].reshape(4 * piece, width), qkv_weight(pack)).reshape(
            4, piece, 2 * piece
        )

    def shape_heads(slot, carry):
        core, chip = slot // 4, slot % 4
        place = place_of(me, core, chip)
        block = raw[core, chip]
        query = block[:, :piece]
        both = block[:, piece:]
        other_way = swapped_halves(both)
        key = jnp.where(low, both, other_way)
        value_out[place] = rounded(jnp.where(low, other_way, both))
        factor = lax.rsqrt(halves_sum(query * query, low) / half_head + epsilon)
        normed = query * factor
        scaled = normed * gain_query
        cos, sin = angle_tables(table, place)
        sin = jnp.where(early, -sin, sin)
        query_out[place] = rounded(scaled * cos + turned(scaled, early) * sin)
        query_normed[place] = normed
        query_factor[place] = factor
        factor = jnp.broadcast_to(mean_square_factor(key), key.shape)
        normed = key * factor
        scaled = normed * gain_key
        key_out[place] = rounded(scaled * cos + turned(scaled, early) * sin)
        key_normed[place] = normed
        key_factor[place] = factor
        return carry

    lax.fori_loop(0, 8, shape_heads, 0)
    copy = pltpu.make_async_copy(held, kept.at[pl.ds(0, 56)], sem)
    copy.start()
    masks = head_masks()
    values_across = value_out[...].reshape(width, piece).T.astype(bf16)
    for block in range(4):
        count = 2 * piece * (block + 1)
        keys = key_out[: 2 * block + 2].reshape(count, piece).astype(bf16)
        score = block_scores(keys, block_queries(query_out, block, masks), count)
        peak = jnp.max(score, axis=0, keepdims=True)
        raised = jnp.exp(score - peak)
        total = jnp.sum(raised, axis=0, keepdims=True)
        chance = (raised * (1.0 / total)).astype(bf16)
        log_out[block] = peak + jnp.log(total)
        result = pick_heads(dot(values_across[:, :count], chance)).astype(bf16)
        for index in range(2):
            attended[slot_of(me, 2 * block + index)] = result[index * piece : (index + 1) * piece]
    copy.wait()


def branch_kernel(info, own, far, near, next_, mine, other, tokens, gains, mixed_out, feed_out, out_rows, attended):
    me = info[1]
    for chip, ref in enumerate((own, far, near, next_)):
        for core in range(2):
            start = pl.multiple_of(place_of(me, core, chip) * piece, piece)
            attended[:, pl.ds(start, piece)] = ref[core]
    rows = attended[...]
    own = pl.ds(pl.multiple_of(me * piece, piece), piece)
    for core, ref in enumerate((mine, other)):
        for chip in range(4):
            start = pl.multiple_of(place_of(me, core, chip) * piece, piece)
            mixed_out[:, pl.ds(start, piece)] = dot(rows, ref[chip])
            out_rows[:, pl.ds(start, piece)] = ref[chip, own, :]
    mixed = tokens[...].astype(f32) + mixed_out[...]
    mixed_out[...] = mixed
    gain = wide_gain(gains, 8)
    feed_out[...] = (mixed * mean_square_factor(mixed) * gain).astype(bf16)


def squash(value):
    return 1.0 / (1.0 + jnp.exp(-value))


def feed_kernel(feed_rows, seed_rows, weight, state, result_out):
    low = lanes() < half_head

    def grads(gate, up, grad):
        squashed = squash(gate)
        activated = gate * squashed
        return (
            grad * up * squashed * (1.0 + gate * (1.0 - squashed)),
            grad * activated,
            activated * up,
        )

    starts = [0, main, 2 * main, 3 * main, 3 * main + piece, packed]

    def step(index, carry):
        blocks = pl.ds(2 * index, 2)
        feed = feed_rows[blocks].reshape(2 * piece, width)
        seed = seed_rows[blocks].reshape(2 * piece, width)
        first = grads(
            dot(feed, weight[:, :main]),
            dot(feed, weight[:, main : 2 * main]),
            dot(seed, weight[:, 2 * main : 3 * main]),
        )
        pair = dot(feed, weight[:, 3 * main : 3 * main + piece])
        rest = grads(pair, swapped_halves(pair), dot(seed, weight[:, 3 * main + piece :]))
        made = [value.astype(bf16) for value in first]
        made.append(jnp.where(low, rest[0], swapped_halves(rest[1])).astype(bf16))
        made.append(jnp.where(low, rest[2], 0.0).astype(bf16))
        for number, value in enumerate(made):
            span = slice(starts[number], starts[number + 1])
            state[blocks, :, span] = value.reshape(2, piece, value.shape[1])
        result = dot_nt(made[0], weight[:, :main]) + dot_nt(made[1], weight[:, main : 2 * main])
        result = result + dot_nt(made[3], weight[:, 3 * main : 3 * main + piece])
        result_out[blocks] = result.astype(bf16).reshape(2, piece, width)
        return carry

    lax.fori_loop(0, 2, step, 0)


def feed_sums_kernel(
    feed_mine, feed_other, seed_mine, seed_other, state_mine, state_other, sums
):
    rows = 4 * piece

    def step(block, carry):
        columns = pl.ds(pl.multiple_of(block * 2 * piece, 2 * piece), 2 * piece)

        def both(mine, other, low, high):
            total = dot_tn(
                mine[:, :, columns].reshape(rows, 2 * piece),
                state_mine[:, :, low:high].reshape(rows, high - low),
            )
            total = total + dot_tn(
                other[:, :, columns].reshape(rows, 2 * piece),
                state_other[:, :, low:high].reshape(rows, high - low),
            )
            sums[columns, low:high] = total.astype(bf16)

        both(feed_mine, feed_other, 0, 2 * main)
        both(seed_mine, seed_other, 2 * main, 3 * main)
        both(feed_mine, feed_other, 3 * main, 3 * main + piece)
        both(seed_mine, seed_other, 3 * main + piece, packed)
        return carry

    lax.fori_loop(0, 4, step, 0)


def feed_out_kernel(state_mine, state_other, weight, keep, give):
    rows = 4 * piece
    for state, ref in ((state_other, give), (state_mine, keep)):
        hidden = state[:, :, 2 * main : 3 * main].reshape(rows, main)
        result = dot_nt(hidden, weight[:, 2 * main : 3 * main])
        hidden = state[:, :, 3 * main + piece :].reshape(rows, piece)
        result = result + dot_nt(hidden, weight[:, 3 * main + piece :])
        ref[...] = result.astype(bf16).reshape(4, piece, width)


def meet_kernel(keep, got, own, far, near, next_):
    for chip, out in enumerate((own, far, near, next_)):
        out[...] = (keep[chip].astype(f32) + got[chip].astype(f32)).astype(bf16)


def grad_mixed_kernel(own, far, near, next_, mixed, seed, gains, grad_out, low_out):
    grad = own[...].astype(f32) + far[...].astype(f32) + near[...].astype(f32) + next_[...].astype(f32)
    x = mixed[...]
    factor = mean_square_factor(x)
    normed = x * factor
    scaled = grad * wide_gain(gains, 8)
    back = factor * (scaled - normed * jnp.mean(scaled * normed, axis=-1, keepdims=True))
    result = seed[...].astype(f32) + back
    grad_out[...] = result
    low_out[...] = result.astype(bf16)


def output_kernel(own, far, near, next_, mixed, out):
    total = own[...].astype(f32) + far[...].astype(f32) + near[...].astype(f32) + next_[...].astype(f32)
    out[...] = (mixed[...] + total).astype(bf16)


def input_kernel(own, far, near, next_, tokens, grad_mixed, gains, out):
    grad = own[...].astype(f32) + far[...].astype(f32) + near[...].astype(f32) + next_[...].astype(f32)
    x = tokens[...].astype(f32)
    factor = mean_square_factor(x)
    normed = x * factor
    scaled = grad * wide_gain(gains, 0)
    back = factor * (scaled - normed * jnp.mean(scaled * normed, axis=-1, keepdims=True))
    out[...] = (grad_mixed[...] + back).astype(bf16)


def backward_kernel(
    info, pack, gains, branch_mine, branch_other, out_rows, table, log_sum, kept,
    keep, give, raw_out, gain_out,
    grads, query_grad, key_grad, value_grad, held, sem,
):
    copy = pltpu.make_async_copy(kept.at[pl.ds(0, 56)], held, sem)
    copy.start()
    queries, keys, values, query_normed, key_normed, query_factor, key_factor = [
        held.at[pl.ds(8 * i, 8)] for i in range(7)
    ]
    me = info[1]
    low = lanes() < half_head
    early = lanes() % half_head < half_head // 2
    gain_query = gains[0:1, piece : 2 * piece]
    gain_key = gains[1:2, piece : 2 * piece]
    for core, ref in enumerate((branch_mine, branch_other)):
        grad = dot_nt(ref[...].reshape(4 * piece, width), out_rows[...]).astype(bf16)
        for chip in range(4):
            grads[place_of(me, core, chip)] = grad[chip * piece : (chip + 1) * piece]
    masks = head_masks()
    copy.wait()
    keys_across = keys[...].reshape(width, piece).T.astype(bf16)
    key_grad[...] = jnp.zeros_like(key_grad)
    value_grad[...] = jnp.zeros_like(value_grad)
    scale = half_head**-0.5
    for block in range(4):
        count = 2 * piece * (block + 1)
        some = 2 * block + 2
        key = keys[:some].reshape(count, piece).astype(bf16)
        value = values[:some].reshape(count, piece).astype(bf16)
        stacked = block_queries(queries, block, masks)
        grad = block_queries(grads, block, masks)
        chance = jnp.exp(block_scores(key, stacked, count) - log_sum[block])
        grad_chance = dot_nt(value, grad)
        inner = jnp.sum(chance * grad_chance, axis=0, keepdims=True)
        grad_score = (chance * (grad_chance - inner)).astype(bf16)
        value_grad[:some] += dot(chance.astype(bf16), grad).reshape(some, piece, piece)
        key_grad[:some] += dot(grad_score, stacked).reshape(some, piece, piece)
        result = pick_heads(dot(keys_across[:, :count], grad_score))
        query_grad[2 * block] = result[:piece]
        query_grad[2 * block + 1] = result[piece:]

    def finish(place, sums):
        cos, sin = angle_tables(table, place)
        sin = jnp.where(early, sin, -sin)

        def turn_back(value):
            return value * cos + turned(value, early) * sin

        grad = turn_back(rounded(query_grad[place] * scale))
        normed = query_normed[place]
        query_sum = sums[0] + jnp.sum(grad * normed, axis=0, keepdims=True)
        scaled = grad * gain_query
        mean = halves_sum(scaled * normed, low) / half_head
        raw_query = query_factor[place] * (scaled - normed * mean)
        both = key_grad[place]
        grad = turn_back(rounded((both + swapped_halves(both)) * scale))
        normed = key_normed[place]
        key_sum = sums[1] + jnp.sum(grad * normed, axis=0, keepdims=True)
        scaled = grad * gain_key
        mean = jnp.mean(scaled * normed, axis=-1, keepdims=True)
        raw_key = key_factor[place] * (scaled - normed * mean)
        both = value_grad[place]
        raw_value = both + swapped_halves(both)
        partner = place ^ me
        core, chip = partner % 2, partner // 2
        raw_out[core, chip, :, :piece] = raw_query.astype(bf16)
        raw_out[core, chip, :, piece:] = jnp.where(low, raw_key, raw_value).astype(bf16)
        return (query_sum, key_sum)

    zero = jnp.zeros((1, piece), f32)
    query_sum, key_sum = lax.fori_loop(0, 8, finish, (zero, zero))
    query_sum = query_sum + swapped_halves(query_sum)
    gain_out[...] = jnp.concatenate([query_sum, key_sum, jnp.zeros((6, piece), f32)], axis=0)
    for core, ref in ((1, give), (0, keep)):
        ref[...] = (
            dot_nt(raw_out[core].reshape(4 * piece, 2 * piece), qkv_weight(pack))
            .astype(bf16)
            .reshape(4, piece, width)
        )


def out_sums_kernel(info, attended, branch_mine, branch_other, sums):
    me = info[1]
    rows = 4 * piece
    total = dot_tn(attended[:4].reshape(rows, piece), branch_mine[...].reshape(rows, width))
    total = total + dot_tn(attended[4:].reshape(rows, piece), branch_other[...].reshape(rows, width))
    total = total.astype(bf16)
    for place in range(8):
        sums[slot_of(me, place)] = total[:, place * piece : (place + 1) * piece]


def pair_kernel(parts, got, own, far, near, next_):
    for chip, out in enumerate((own, far, near, next_)):
        out[0] = parts[chip]
        out[1] = got[chip]


def attention_sums_kernel(info, mixer, raw, own, far, near, next_, gain_sums, sums):
    total = dot_tn(mixer[...].reshape(width, width), raw[...].reshape(width, 2 * piece))
    sums[:, :half_head, : 2 * piece] = total.astype(bf16).reshape(16, half_head, 2 * piece)
    me = info[1]
    for chip, ref in enumerate((own, far, near, next_)):
        for core in range(2):
            place = place_of(me, core, chip)
            for index in range(2):
                block = ref[core, index * half_head : (index + 1) * half_head, :]
                sums[2 * place + index, :half_head, 2 * piece :] = block
    value = gain_sums[...]
    high = value.astype(bf16).astype(f32)
    tail = jnp.concatenate([high, value - high], axis=0)
    tail = jnp.concatenate([tail, jnp.zeros((16, 2 * piece), f32)], axis=1).astype(bf16)
    for index in range(16):
        sums[index, half_head:, :] = tail


def feed_total_kernel(parts, total, low):
    value = parts[0].astype(f32)
    for index in range(1, 16):
        value = value + parts[index].astype(f32)
    total[...] = value
    low[...] = value.astype(bf16)


def feed_outputs_kernel(info, own, other, gate, up, down):
    context = info[2]
    late = context == 1
    low = lanes() < half_head
    here = pl.multiple_of(context * main, main)
    there = pl.multiple_of((1 - context) * main, main)
    for index, ref in enumerate((gate, up, down)):
        span = slice(index * main, (index + 1) * main)
        ref[:, pl.ds(here, main)] = own[:, span].astype(f32)
        ref[:, pl.ds(there, main)] = other[:, span].astype(f32)
    span = slice(3 * main, 3 * main + piece)
    mine, far = own[:, span].astype(f32), other[:, span].astype(f32)
    first, second = jnp.where(late, far, mine), jnp.where(late, mine, far)
    gate[:, 2 * main :] = jnp.where(low, first, swapped_halves(second))
    up[:, 2 * main :] = jnp.where(low, swapped_halves(first), second)
    span = slice(3 * main + piece, packed)
    mine, far = own[:, span].astype(f32), other[:, span].astype(f32)
    first, second = jnp.where(late, far, mine), jnp.where(late, mine, far)
    down[:, 2 * main :] = jnp.where(low, first, swapped_halves(second))


def attention_total_kernel(parts, pack, feed_pack, feed_total, final):
    value = parts[0].astype(f32)
    for index in range(1, 16):
        value = value + parts[index].astype(f32)
    weights = value[:half_head]
    tail = value[half_head : half_head + 8, :piece] + value[half_head + 8 :, :piece]
    first = jnp.sum(
        pack[...].astype(f32) * weights[:, : 2 * piece],
        axis=1,
        keepdims=True,
    )
    feed = jnp.sum(
        feed_pack[:, : 2 * main].astype(f32) * feed_total[:, : 2 * main].astype(f32), axis=1, keepdims=True
    )
    span = slice(3 * main, 3 * main + piece)
    feed = feed + jnp.sum(
        feed_pack[:, span].astype(f32) * feed_total[:, span].astype(f32), axis=1, keepdims=True
    )
    lane = lanes(half_head)
    spread = jnp.where(lane == 0, first, jnp.where(lane == 1, feed, 0.0))
    spread = jnp.concatenate([spread, jnp.zeros_like(spread)], axis=0).T
    rows = jnp.concatenate([spread[:8], tail], axis=0)
    rows = jnp.concatenate([rows, jnp.zeros((16, 2 * piece), f32)], axis=1)
    result = jnp.concatenate([weights, rows], axis=0).astype(bf16)
    for index in range(8):
        final[index] = result


def attention_outputs_kernel(small, final, query, key, value, out, gains):
    low = lanes() < half_head
    for place in range(8):
        span = slice(place * piece, (place + 1) * piece)
        query[:, span] = final[place, :half_head, :piece].astype(f32)
        out[:, span] = final[place, :half_head, 2 * piece :].astype(f32)
    for pair in range(4):
        span = slice(pair * piece, (pair + 1) * piece)
        first = final[2 * pair, :half_head, piece : 2 * piece].astype(f32)
        second = final[2 * pair + 1, :half_head, piece : 2 * piece].astype(f32)
        key[:, span] = jnp.where(low, first, swapped_halves(second))
        value[:, span] = jnp.where(low, swapped_halves(first), second)
    tail = final[0, half_head:, :piece].astype(f32)
    for place in range(1, 8):
        tail = tail + final[place, half_head:, :piece].astype(f32)
    both = small[0:1, :]
    gains[0:1] = tail[0:1] / both
    gains[1:2] = tail[1:2] / swapped_halves(both)
    gains[2:4] = tail[8:10]


def swap(value, bits):
    return lax.ppermute(value, line, [(i, i ^ bits) for i in range(8)])


def line_gather(block, *others):
    far, near, next_ = swap(block, 2), swap(block, 4), swap(block, 6)
    mine = jnp.stack([after(block, *others), far, near, next_])
    return mine, swap(mine, 1)


def line_reduce(keep, give, *others):
    got = swap(give, 1)
    keep = after(keep, *others)
    sent = call(meet_kernel, [shape((piece, width), bf16)] * 4, keep, got, micros=2, name="meet")
    return sent[0], swap(sent[1], 2), swap(sent[2], 4), swap(sent[3], 6)


def line_turn(parts):
    got = swap(parts[4:], 1)
    pair = shape((2,) + parts.shape[1:], parts.dtype)
    sent = call(pair_kernel, [pair] * 4, parts, got, micros=1, name="pair")
    return sent[0], swap(sent[1], 2), swap(sent[2], 4), swap(sent[3], 6)


def after(value, *others):
    return lax.optimization_barrier((value,) + others)[0]


def across(value):
    return lax.all_to_all(value, "shard", 0, 0, tiled=True)


def rope_table():
    frequency = rope_base ** (-np.arange(0, half_head, 2) / half_head)
    frequency = np.concatenate([frequency] * 4)[None, :]
    starts = np.arange(8)[:, None] * piece * frequency
    steps = np.arange(piece)[:, None] * frequency
    rows = [np.cos(starts), np.sin(starts), np.cos(steps), np.sin(steps)]
    return jnp.asarray(np.concatenate(rows), f32)


def on_device(
    tokens,
    cotangent,
    attention_gain,
    query_weight,
    key_weight,
    value_weight,
    query_gain,
    key_gain,
    out_weight,
    feed_gain,
    gate_weight,
    up_weight,
    down_weight,
):
    shard = lax.axis_index("shard")
    context = lax.axis_index("context")
    place = context * 4 + lax.axis_index("tensor")
    info = jnp.stack([shard, place, context]).astype(jnp.int32)
    token_rows = tokens.reshape(piece, width)
    seed_rows = cotangent.reshape(piece, width)
    gains = [value.reshape(1, -1) for value in (attention_gain, feed_gain, query_gain, key_gain)]
    pack, own_pack, small = call(
        pack_kernel,
        [
            shape((16, 80, 3 * piece), bf16),
            shape((half_head, 2 * piece), bf16),
            shape((8, piece), f32),
        ],
        info, *gains, query_weight, key_weight, value_weight, out_weight,
        micros=6,
        name="pack",
        fetch=True,
    )
    feed_pack, own_feed = call(
        feed_pack_kernel,
        [shape((16, half_head, packed), bf16), shape((half_head, packed), bf16)],
        info, gate_weight, up_weight, down_weight.T,
        micros=12,
        name="feed_pack",
        fetch=True,
    )
    pack = after(across(pack), feed_pack)
    feed_full = across(after(feed_pack, pack)).reshape(width, packed)
    out_columns = pack[:, :half_head, 2 * piece :].reshape(width, piece)
    tokens_mine, tokens_other = line_gather(token_rows, own_pack)
    seed_mine, seed_other = line_gather(after(seed_rows, tokens_mine))
    table = rope_table()
    cube = (8, piece, piece)
    attended_heads, mixer, log_sum, gains, kept = call(
        forward_kernel,
        [
            shape(cube, bf16), shape((2, 4, piece, width), bf16), shape((4, 1, 4 * piece), f32),
            shape((16, 3 * piece), f32), shape((1100, piece, piece), f32),
        ],
        info, pack, after(tokens_mine, seed_mine), tokens_other, table,
        micros=36,
        scratch=[
            pltpu.VMEM((2, 4, piece, 2 * piece), f32),
            pltpu.VMEM((56, piece, piece), f32),
            pltpu.SemaphoreType.DMA,
        ],
        name="attention_forward",
    )
    out_mine, out_other = line_gather(out_columns, attended_heads)
    attended = line_turn(attended_heads)
    mixed, feed_input, out_rows = call(
        branch_kernel,
        [shape((piece, width), f32), shape((piece, width), bf16), shape((piece, width), bf16)],
        info, *attended, out_mine, out_other, token_rows, gains,
        micros=2,
        scratch=[pltpu.VMEM((piece, width), bf16)],
        name="branch",
    )
    feed_mine, feed_other = line_gather(feed_input, feed_full)
    rows = (feed_mine, feed_other, seed_mine, seed_other)
    line_shape = shape((4, piece, width), bf16)
    halves = [shape((4, piece, packed), bf16), line_shape]
    state_mine, grad_keep = call(
        feed_kernel, halves, feed_mine, seed_mine, feed_full, micros=6, name="feed_forward"
    )
    state_other, grad_give = call(
        feed_kernel,
        halves,
        feed_other, after(seed_other, grad_keep), feed_full,
        micros=6,
        name="feed_forward",
    )
    grad_feed = line_reduce(grad_keep, grad_give)
    (sums,) = call(
        feed_sums_kernel,
        [shape((width, packed), bf16)],
        *rows, state_mine, state_other,
        micros=8,
        name="feed_sums",
    )
    feed_parts = across(sums.reshape(16, half_head, packed))
    grad_mixed, grad_branch = call(
        grad_mixed_kernel,
        [shape((piece, width), f32), shape((piece, width), bf16)],
        after(grad_feed[0], sums), *grad_feed[1:], mixed, seed_rows, gains,
        name="grad_mixed",
    )
    (out_keep, out_give) = call(
        feed_out_kernel,
        [line_shape, line_shape],
        after(state_mine, grad_branch), state_other, feed_full,
        micros=4,
        name="feed_out",
    )
    branch_mine, branch_other = line_gather(grad_branch, out_keep)
    (out_parts,) = call(
        out_sums_kernel,
        [shape(cube, bf16)],
        info, attended_heads, branch_mine, branch_other,
        micros=1,
        name="out_sums",
    )
    out_sums = line_turn(out_parts)
    cube_f32 = pltpu.VMEM(cube, f32)
    mixer_keep, mixer_give, raw, gain_sums = call(
        backward_kernel,
        [
            shape((4, piece, width), bf16),
            shape((4, piece, width), bf16),
            shape((2, 4, piece, 2 * piece), bf16),
            shape((8, piece), f32),
        ],
        info, pack, gains, branch_mine, branch_other, after(out_rows, out_parts), table, log_sum, kept,
        micros=6,
        scratch=[
            pltpu.VMEM(cube, bf16), cube_f32, cube_f32, cube_f32,
            pltpu.VMEM((56, piece, piece), f32), pltpu.SemaphoreType.DMA,
        ],
        name="attention_backward",
    )
    (attention_sums,) = call(
        attention_sums_kernel,
        [shape((16, 80, 3 * piece), bf16)],
        info, mixer, raw, *out_sums, gain_sums,
        micros=2,
        name="attention_sums",
    )
    grad_mixer = line_reduce(mixer_keep, mixer_give)
    attention_parts = across(after(attention_sums, *grad_mixer[1:]))
    feed_total, feed_low = call(
        feed_total_kernel,
        [shape((half_head, packed), f32), shape((half_head, packed), bf16)],
        after(feed_parts, attention_sums),
        name="feed_total",
    )
    (input_gradient,) = call(
        input_kernel,
        [shape((piece, width), bf16)],
        *grad_mixer, token_rows, grad_mixed, gains,
        name="input_gradient",
        store=True,
    )
    (output,) = call(
        output_kernel,
        [shape((piece, width), bf16)],
        *line_reduce(out_keep, after(out_give, raw)), mixed,
        name="output",
        store=True,
    )
    feed_far = swap(feed_low, 4)
    long = shape((half_head, 2 * main + piece), f32)
    gate_part, up_part, down_part = call(
        feed_outputs_kernel, [long, long, long], info, feed_total, feed_far, name="feed_outputs", store=True
    )
    (final,) = call(
        attention_total_kernel,
        [shape((8, 80, 3 * piece), bf16)],
        attention_parts, own_pack, own_feed, feed_total,
        name="attention_total",
    )
    final = lax.all_to_all(final, line, 0, 0, tiled=True)
    query_part, key_part, value_part, out_part, gain_parts = call(
        attention_outputs_kernel,
        [
            shape((half_head, width), f32), shape((half_head, main), f32),
            shape((half_head, main), f32), shape((half_head, width), f32), shape((4, piece), f32),
        ],
        small, final,
        name="attention_outputs", store=True,
    )
    head_gains = lax.dynamic_slice(gain_parts, (2, 4 * shard), (2, 4))
    return (
        output.reshape(1, piece, width),
        input_gradient.reshape(1, piece, width),
        gain_parts[0, :half_head],
        query_part,
        key_part,
        value_part,
        head_gains[0],
        head_gains[1],
        out_part,
        gain_parts[1, :half_head],
        gate_part,
        up_part,
        down_part.T,
    )


def solution(mesh):
    tokens = P("shard", ("context", "tensor"), None)
    rows = P("shard", None)
    weights = (P("shard"), rows, rows, rows, P("shard"), P("shard"), rows, P("shard")) + (
        P("shard", "tensor"),
        P("shard", "tensor"),
        P("tensor", "shard"),
    )
    placed = (tokens, tokens) + weights
    return jax.shard_map(
        on_device, mesh=mesh, in_specs=placed, out_specs=placed, check_vma=False
    )
```
